256 devices in a mesh: aux: 16 (over y_lo, z), row: 16 (over x, y_hi, core).
Axes of the slice: x: 4, y: 4 (y_hi: 2, y_lo: 2; y = y_hi * 2 + y_lo), z: 8, core: 2. Of those that a mesh axis runs over, the one named last changes fastest.
Arguments:
- three_index: float32 [192, 2048, 512], P('aux', 'row'), may hold values from -0.40296373 to 0.40296373
- coefficients: float32 [2048, 256], P('aux'), may hold values from -0.25 to 0.25
- tile_index: int32 [16, 16, 4], P('aux', 'row'), may hold values from 0 to 15, as said below
Outputs:
- exchange_matrix: float32 [2048, 2048], P('row', 'aux')
The draws below stay inside these ranges and needn't reach their ends.
Inputs may be any that keep to these rules, and one draw needn't show every extreme that they name: `tile_index`: the 4 tiles of one block are distinct.
All inputs are finite; a program needn't handle non-finite values.
Results may differ from the reference program's by a relative error of at most 0.00005.
Values sent between devices are 32-bit elements; how exact they have to be, the bound alone decides.
A program may use at most 128 MiB of HBM per device.

```python
import jax
import jax.numpy as jnp
from jax import lax

NB = 2048
NOCC = 256
TILE = 128
NT = 4
AUX_DEV = 12
NAUX = 192
MROWS = 128
N_AUX = 16
N_ROW = 16


def draw_tile_index(key, part):
    key = jax.random.fold_in(key, 7)
    count = NB // TILE
    keys = jax.random.split(key, N_AUX * N_ROW)
    perms = jax.vmap(lambda k: jax.random.permutation(k, count))(keys)[:, :NT].astype(jnp.int32)
    first = jnp.concatenate([jnp.array([0, count - 1], dtype=jnp.int32), jnp.arange(1, NT - 1, dtype=jnp.int32)])
    perms = perms.at[0].set(first)
    return perms.reshape(N_AUX, N_ROW, NT)


def level_of(stream_key, dims, cuts, low, largest):
    gain, own = 1.0, jax.random.fold_in(stream_key, 6)
    for axis_at, blocks in cuts:
        steps = jnp.exp(jax.random.uniform(jax.random.fold_in(own, axis_at), (blocks,), jnp.float32, low / len(cuts), largest / len(cuts)))
        gain = gain * jnp.repeat(steps, dims[axis_at] // blocks).reshape([-1 if axis == axis_at else 1 for axis in range(len(dims))])
    return gain


def normal_values(key, dims, spread, reach, pieces=(), held_as=jnp.bfloat16):
    entries = jax.random.normal(key, dims, jnp.float32) * spread
    if len(pieces) > 0:
        entries = level_of(key, dims, pieces, -0.22, 0.18) * entries
    return jnp.clip(entries, min=-reach, max=reach).astype(held_as)


def setup_inputs(seed: int = 0) -> dict:
    arg_keys = jax.random.split(jax.random.key(seed), 4)
    return {
        "three_index": normal_values(arg_keys[0], (NAUX, NB, NT * TILE), ((NAUX * NOCC) ** -0.25), 0.40296373, ((0, 16), (1, 16)), jnp.float32),
        "coefficients": normal_values(arg_keys[1], (NB, NOCC), (NT * TILE) ** -0.5, 0.25, ((0, 16),), jnp.float32),
        "tile_index": draw_tile_index(jax.random.fold_in(arg_keys[3], 71), 0),
    }


def reference(three_index, coefficients, tile_index):
    offsets = jnp.arange(TILE, dtype=jnp.int32)
    row_ids = (tile_index[:, :, :, None] * TILE + offsets).reshape(N_AUX, N_ROW, NT * TILE)
    selected = coefficients[row_ids]
    blocks = three_index.reshape(N_AUX, AUX_DEV, N_ROW, MROWS, NT * TILE)
    half = jnp.einsum("apbmk,abki->apbmi", blocks, selected, precision=lax.Precision.HIGHEST)
    flat = half.reshape(NAUX, NB, NOCC).transpose(1, 0, 2).reshape(NB, NAUX * NOCC)
    return jnp.dot(flat, flat.T, precision=lax.Precision.HIGHEST, preferred_element_type=jnp.float32)
```

```python
import functools

import jax
import jax.numpy as jnp
from jax import lax
from jax.experimental import pallas as pl
from jax.experimental.pallas import tpu as pltpu
from jax.sharding import PartitionSpec as P

MESH = pl.DeviceIdType.MESH
F32 = jnp.float32
BF16 = jnp.bfloat16
NT_DIMS = (((1,), (1,)), ((), ()))
NN_DIMS = (((1,), (0,)), ((), ()))


def split(value):
    high = value.astype(BF16)
    return high, (value - high.astype(F32)).astype(BF16)


def dot3(lh, ll, rh, rl, dims):
    dot = functools.partial(lax.dot_general, dimension_numbers=dims, preferred_element_type=F32)
    return dot(lh, rh) + (dot(lh, rl) + dot(ll, rh))


def kernel(
    x_ref, c_ref, t_ref, out_ref,
    xh, xl, tslice, tvec, tall, tsm, picks, csel, ch, cl,
    hb, blk, xfull, xhalf, gg, eh, part, ry, summed, rz, red, fin,
    c1s, c1r, tis, tir, c2s, c2r, tsem, has, har, xs, xr, rys, ryr, rzs, rzr, fs, fr,
):
    a = lax.axis_index("aux")
    r = lax.axis_index("row")
    lo, z = a // 8, a % 8
    x, i = r // 4, r % 4
    hi, c = i // 2, i % 2
    y = hi * 2 + lo

    def at(px, py, pz, pc):
        return (py % 2) * 8 + pz, px * 4 + (py // 2) * 2 + pc

    def remote(src, dst, ss, rs, dev):
        return pltpu.make_async_remote_copy(
            src_ref=src, dst_ref=dst, send_sem=ss, recv_sem=rs, device_id=dev, device_id_type=MESH
        )

    def is_me(dev):
        return (dev[0] == a) & (dev[1] == r)

    e = z % 2
    bi, bj = y, z // 2
    fa_row = lax.rem(x + 4 - c, 4)
    fa_col = lax.rem(fa_row + 1, 4)
    ea, eb = lax.rem(x + 3, 4), lax.rem(x + 1, 4)
    outgoing = [
        (0, 0, (x * 4 + bj, x * 4 + bi)),
        (1, 0, (fa_col * 4 + bj, fa_row * 4 + bi)),
        (1, 1, (fa_row * 4 + bi, fa_col * 4 + bj)),
        (2, 0, (eb * 4 + bj, ea * 4 + bi)),
        (2, 1, (ea * 4 + bi, eb * 4 + bj)),
    ]
    xc, jc = a // 4, a % 4
    delta = lax.rem(xc + 4 - x, 4)
    has_plain = delta <= 2
    has_turned = delta >= 2
    incoming = []
    for sc in (0, 1):
        plain_x = jnp.where(delta == 0, x, jnp.where(delta == 1, x if sc == 0 else xc, lax.rem(x + 1, 4)))
        turned_x = jnp.where(delta == 3, xc if sc == 0 else x, lax.rem(x + 3, 4))
        for se in (0, 1):
            incoming.append((0, sc, se, has_plain, at(plain_x, i, 2 * jc + se, sc)))
            incoming.append((1, sc, se, has_turned, at(turned_x, jc, 2 * i + se, sc)))

    barrier = pltpu.get_barrier_semaphore()

    def greet(dev):
        pl.semaphore_signal(barrier, inc=1, device_id=dev, device_id_type=MESH)

    def greet_axes(d, _):
        greet((a, lax.rem(r + d, 16)))
        greet((lax.rem(a + d, 16), r))
        return 0

    lax.fori_loop(1, 16, greet_axes, 0)
    greet(at(x, 3 - y, z, c))
    for _, _, _, there, dev in incoming:
        @pl.when(there & jnp.logical_not(is_me(dev)))
        def _():
            greet(dev)
    expect = 31
    for _, _, dev in outgoing:
        expect = expect + jnp.where(is_me(dev), 0, 1)

    lane = lax.broadcasted_iota(jnp.int32, (8, 128), 1)
    ids = jnp.zeros((8, 128), jnp.int32)
    for s in range(4):
        ids = jnp.where(lane == s, t_ref[0, 0, s], ids)
    tvec[...] = ids
    pl.semaphore_wait(barrier, expect)

    def c1(d):
        return remote(c_ref.at[lax.rem(r, 16)], tslice.at[a], c1s.at[d - 1], c1r.at[d - 1], (lax.rem(a + d, 16), r))

    def c1_in(d):
        return remote(c_ref.at[r], tslice.at[lax.rem(a + 16 - d, 16)], c1s.at[d - 1], c1r.at[d - 1], (a, r))

    def ti(d):
        return remote(tvec, tall.at[r], tis.at[d - 1], tir.at[d - 1], (a, lax.rem(r + d, 16)))

    def ti_in(d):
        return remote(tvec, tall.at[lax.rem(r + 16 - d, 16)], tis.at[d - 1], tir.at[d - 1], (a, r))

    def start1(d, _):
        c1(d).start()
        ti(d).start()
        return 0

    lax.fori_loop(1, 16, start1, 0)
    tslice[a] = c_ref[r]
    tall[r] = ids

    def split_x(n, _):
        rows = pl.ds(pl.multiple_of(n * 128, 128), 128)
        high, low = split(x_ref[rows, :])
        xh[rows, :] = high
        xl[rows, :] = low
        return 0

    lax.fori_loop(0, 12, split_x, 0)

    def wait1(d, _):
        ti_in(d).wait_recv()
        return 0

    lax.fori_loop(1, 16, wait1, 0)
    to_smem = pltpu.make_async_copy(tall.at[:, 0], tsm, tsem)
    to_smem.start()
    to_smem.wait()

    def wait1c(d, _):
        c1_in(d).wait_recv()
        return 0

    lax.fori_loop(1, 16, wait1c, 0)

    def c2(d):
        return remote(picks.at[d - 1], csel.at[:, r], c2s.at[d - 1], c2r.at[d - 1], (a, lax.rem(r + d, 16)))

    def c2_in(d):
        return remote(picks.at[d - 1], csel.at[:, lax.rem(r + 16 - d, 16)], c2s.at[d - 1], c2r.at[d - 1], (a, r))

    def start2(d, _):
        who = lax.rem(r + d, 16)
        for s in range(4):
            picks[d - 1, s] = tslice[tsm[who, s]]
        c2(d).start()
        return 0

    lax.fori_loop(1, 16, start2, 0)
    for s in range(4):
        csel[s, r] = tslice[tsm[r, s]]

    def wait2(d, _):
        c2_in(d).wait_recv()
        return 0

    lax.fori_loop(1, 16, wait2, 0)
    for s in range(4):
        high, low = split(csel[s].reshape(128, 256))
        ch[s * 128:(s + 1) * 128, :] = high
        cl[s * 128:(s + 1) * 128, :] = low

    peers = [lax.rem(i + 2, 4), 3 - i, i + 1 - 2 * c]

    def swap(k):
        return remote(hb.at[k], blk.at[:, i], has.at[k], har.at[k], (a, x * 4 + peers[k]))

    def swap_in(k):
        return remote(hb.at[k], blk.at[:, peers[k]], has.at[k], har.at[k], (a, r))

    def half_of(g):
        rows = pl.ds(pl.multiple_of(g * 384, 128), 384)
        return dot3(xh[rows, :], xl[rows, :], ch[...], cl[...], NN_DIMS)

    for k in range(3):
        value = half_of(peers[k])
        for q in range(6):
            hb[k, q] = value[(q // 2) * 128:(q // 2 + 1) * 128, (q % 2) * 128:(q % 2 + 1) * 128]
        swap(k).start()
    value = half_of(i)
    for q in range(6):
        blk[q, i] = value[(q // 2) * 128:(q // 2 + 1) * 128, (q % 2) * 128:(q % 2 + 1) * 128]

    step = 2 * c - 1
    x_to = lax.rem(x + 4 + step, 4)
    x_back = lax.rem(x + 4 - step, 4)
    mine = x // 2
    others = x_to // 2

    def xsend(p, k, m):
        first = 3 * (1 - mine)
        second = 3 * mine
        if m == 0:
            return remote(blk.at[pl.ds(first, 3), p], xfull.at[pl.ds(first, 3), p], xs.at[k, 0], xr.at[k, 0], (a, x_to * 4 + i))
        if m == 1:
            return remote(blk.at[pl.ds(second, 3), p], xhalf.at[:, p], xs.at[k, 1], xr.at[k, 1], (a, x_back * 4 + i))
        return remote(blk.at[pl.ds(second, 3), p], xfull.at[pl.ds(second, 3), p], xs.at[k, 2], xr.at[k, 2], (a, x_to * 4 + i))

    def xrecv(p, k, m):
        first = 3 * others
        second = 3 * (1 - others)
        if m == 0:
            return remote(blk.at[pl.ds(first, 3), p], xfull.at[pl.ds(first, 3), p], xs.at[k, 0], xr.at[k, 0], (a, r))
        if m == 1:
            return remote(blk.at[pl.ds(0, 3), p], xhalf.at[:, p], xs.at[k, 1], xr.at[k, 1], (a, r))
        return remote(blk.at[pl.ds(second, 3), p], xfull.at[pl.ds(second, 3), p], xs.at[k, 2], xr.at[k, 2], (a, r))

    pieces = [(i, 3), (peers[2], 2), (peers[0], 0), (peers[1], 1)]
    for p, k in pieces:
        if k != 3:
            swap_in(k).wait_recv()
        for m in range(3):
            xsend(p, k, m).start()

    def turn(src, slot):
        def body(n, _):
            rows = pl.ds(pl.multiple_of(n * 128, 128), 128)
            for q in range(6):
                high, low = split(src[q, n])
                gg[slot, 0, rows, q * 128:(q + 1) * 128] = high
                gg[slot, 1, rows, q * 128:(q + 1) * 128] = low
            return 0
        lax.fori_loop(0, 4, body, 0)

    def turn_half(src, start, slot):
        def body(n, _):
            rows = pl.ds(pl.multiple_of(n * 128, 128), 128)
            for q in range(3):
                high, low = split(src[start + q, n])
                eh[slot, 0, rows, q * 128:(q + 1) * 128] = high
                eh[slot, 1, rows, q * 128:(q + 1) * 128] = low
            return 0
        lax.fori_loop(0, 4, body, 0)

    def products(t, buf, left, right):
        for jj in range(2):
            cols = slice(jj * 256, (jj + 1) * 256)
            value = dot3(buf[left, 0], buf[left, 1], buf[right, 0, cols, :], buf[right, 1, cols, :], NT_DIMS)
            for n in range(4):
                for jl in range(2):
                    for h in range(2):
                        part[t, n, (2 * jj + jl) * 2 + h] = value[
                            n * 128 + h * 64:n * 128 + (h + 1) * 64, jl * 128:(jl + 1) * 128
                        ]

    def ysend(t, d):
        py = lax.rem(y + d, 4)
        return remote(part.at[t, py], ry.at[t, d - 1], rys.at[t, d - 1], ryr.at[t, d - 1], at(x, py, z, c))

    def zsend(t, d):
        pz = lax.rem(z + d, 8)
        return remote(summed.at[t, pz], rz.at[t, d - 1], rzs.at[t, d - 1], rzr.at[t, d - 1], at(x, y, pz, c))

    def y_start(t):
        for d in (2, 1, 3):
            ysend(t, d).start()

    def y_done(t):
        for d in (1, 2, 3):
            ysend(t, d).wait_recv()
        summed[t] = part[t, y] + ry[t, 0] + ry[t, 1] + ry[t, 2]
        for d in (4, 3, 5, 2, 6, 1, 7):
            zsend(t, d).start()

    def z_done(t):
        for d in range(1, 8):
            zsend(t, d).wait_recv()
        total = summed[t, z]
        for d in range(7):
            total = total + rz[t, d]
        red[t] = total

    def deliver(n):
        t, turned, dev = outgoing[n]
        return remote(red.at[t], fin.at[turned, c, e], fs.at[n], fr.at[turned, c, e], dev)

    def send_out(n):
        t, turned, dev = outgoing[n]

        @pl.when(jnp.logical_not(is_me(dev)))
        def _():
            deliver(n).start()

        @pl.when(is_me(dev))
        def _():
            fin[turned, c, e] = red[t]

    turn(blk, c)
    products(0, gg, c, c)
    y_start(0)
    for p, k in pieces:
        xrecv(p, k, 0).wait_recv()
        xrecv(p, k, 1).wait_recv()
    turn_half(xhalf, 0, c)
    turn_half(xfull, 3 * others, 1 - c)
    products(2, eh, 0, 1)
    y_start(2)
    y_done(0)
    for p, k in pieces:
        xrecv(p, k, 2).wait_recv()
    turn(xfull, 1 - c)
    products(1, gg, 0, 1)
    y_start(1)
    y_done(2)
    z_done(0)
    send_out(0)
    y_done(1)
    z_done(2)
    send_out(3)
    send_out(4)
    z_done(1)
    send_out(1)
    send_out(2)

    for turned, sc, se, there, dev in incoming:
        @pl.when(there & jnp.logical_not(is_me(dev)))
        def _():
            remote(red.at[0], fin.at[turned, sc, se], fs.at[0], fr.at[turned, sc, se], (a, r)).wait_recv()

    def gathered(turned):
        return (fin[turned, 0] + fin[turned, 1]).reshape(128, 128)

    @pl.when(delta <= 1)
    def _():
        out_ref[...] = gathered(0)

    @pl.when(delta == 2)
    def _():
        out_ref[...] = gathered(0) + gathered(1).T

    @pl.when(delta == 3)
    def _():
        out_ref[...] = gathered(1).T

    def drain(d, _):
        c1(d).wait_send()
        ti(d).wait_send()
        c2(d).wait_send()
        return 0

    lax.fori_loop(1, 16, drain, 0)
    for k in range(3):
        swap(k).wait_send()
    for p, k in pieces:
        for m in range(3):
            xsend(p, k, m).wait_send()
    for t in range(3):
        for d in range(1, 4):
            ysend(t, d).wait_send()
        for d in range(1, 8):
            zsend(t, d).wait_send()
    for n in range(5):
        @pl.when(jnp.logical_not(is_me(outgoing[n][2])))
        def _():
            deliver(n).wait_send()


def on_device(three_index, coefficients, tile_index):
    dma = pltpu.SemaphoreType.DMA
    vm = pltpu.VMEM
    return pl.pallas_call(
        kernel,
        out_shape=jax.ShapeDtypeStruct((128, 128), F32),
        in_specs=[
            pl.BlockSpec(memory_space=pltpu.VMEM),
            pl.BlockSpec(memory_space=pltpu.VMEM),
            pl.BlockSpec(memory_space=pltpu.SMEM),
        ],
        out_specs=pl.BlockSpec(memory_space=pltpu.VMEM),
        scratch_shapes=[
            vm((1536, 512), BF16), vm((1536, 512), BF16),
            vm((16, 8, 256), F32), vm((8, 128), jnp.int32), vm((16, 8, 128), jnp.int32),
            pltpu.SMEM((16, 128), jnp.int32),
            vm((15, 4, 8, 256), F32), vm((4, 16, 8, 256), F32),
            vm((512, 256), BF16), vm((512, 256), BF16),
            vm((3, 6, 128, 128), F32), vm((6, 4, 128, 128), F32), vm((6, 4, 128, 128), F32), vm((3, 4, 128, 128), F32),
            vm((2, 2, 512, 768), BF16), vm((2, 2, 512, 384), BF16),
            vm((3, 4, 8, 64, 128), F32), vm((3, 3, 8, 64, 128), F32), vm((3, 8, 64, 128), F32),
            vm((3, 7, 64, 128), F32), vm((3, 64, 128), F32), vm((2, 2, 2, 64, 128), F32),
            dma((15,)), dma((15,)), dma((15,)), dma((15,)), dma((15,)), dma((15,)), dma,
            dma((3,)), dma((3,)), dma((4, 3)), dma((4, 3)),
            dma((3, 3)), dma((3, 3)), dma((3, 7)), dma((3, 7)), dma((5,)), dma((2, 2, 2)),
        ],
        compiler_params=pltpu.CompilerParams(
            collective_id=0, has_side_effects=True, vmem_limit_bytes=56 * 2**20
        ),
    )(three_index.reshape(1536, 512), coefficients.reshape(16, 8, 256), tile_index)


def solution(mesh):
    return jax.shard_map(
        on_device,
        mesh=mesh,
        in_specs=(P("aux", "row", None), P("aux", None), P("aux", "row", None)),
        out_specs=P("row", "aux"),
        check_vma=False,
    )
```

```python
import functools

import jax
import jax.numpy as jnp
from jax import lax
from jax.experimental import pallas as pl
from jax.experimental.pallas import tpu as pltpu
from jax.sharding import PartitionSpec as P

MESH = pl.DeviceIdType.MESH
F32 = jnp.float32
BF16 = jnp.bfloat16
NT_DIMS = (((1,), (1,)), ((), ()))
NN_DIMS = (((1,), (0,)), ((), ()))


def split(value):
    high = value.astype(BF16)
    return high, (value - high.astype(F32)).astype(BF16)


def dot3(lh, ll, rh, rl, dims):
    dot = functools.partial(lax.dot_general, dimension_numbers=dims, preferred_element_type=F32)
    return dot(lh, rh) + (dot(lh, rl) + dot(ll, rh))


def kernel(
    x_ref, c_ref, t_ref, out_ref,
    xv, xh, xl, tslice, tvec, tall, tsm, picks, csel, ch, cl,
    hb, blk, xfull, xhalf, gg, eh,
    pc, cb, pf, ryf, sf, rzf, redf, rye, se_, rze, rzd, sd, ryd, redq, fin_q, fin_f,
    loads, c1s, c1r, tis, tir, c2s, c2r, tsem, has, har, xs, xr, ccs, ccr,
    fys, fyr, fzs, fzr, eys, eyr, ezs, ezr, dys, dyr, dzs, dzr, fs, frq, frf,
):
    a = lax.axis_index("aux")
    r = lax.axis_index("row")
    lo, z = a // 8, a % 8
    x, i = r // 4, r % 4
    hi, c = i // 2, i % 2
    y = hi * 2 + lo

    def at(px, py, pz, pc):
        return (py % 2) * 8 + pz, px * 4 + (py // 2) * 2 + pc

    def remote(src, dst, ss, rs, dev):
        return pltpu.make_async_remote_copy(
            src_ref=src, dst_ref=dst, send_sem=ss, recv_sem=rs, device_id=dev, device_id_type=MESH
        )

    def is_me(dev):
        return (dev[0] == a) & (dev[1] == r)

    def load_x(n):
        return pltpu.make_async_copy(x_ref.at[pl.ds(n * 384, 384)], xv.at[pl.ds(n * 384, 384)], loads.at[n])

    for n in range(4):
        load_x(n).start()

    sub = z % 2
    bi, bj = y, z // 2
    step = 2 * c - 1
    x_to = lax.rem(x + 4 + step, 4)
    x_back = lax.rem(x + 4 - step, 4)
    ea, eb = lax.rem(x + 3, 4), lax.rem(x + 1, 4)
    outgoing = [
        ((x * 4 + bj, x * 4 + bi), redq.at[0], fin_q.at[0, c, sub], frq.at[0, c, sub]),
        ((x_back * 4 + bj, x * 4 + bi), redf, fin_f.at[0, sub], frf.at[0, sub]),
        ((x * 4 + bi, x_back * 4 + bj), redf, fin_f.at[1, sub], frf.at[1, sub]),
        ((eb * 4 + bj, ea * 4 + bi), redq.at[1], fin_q.at[0, c, sub], frq.at[0, c, sub]),
        ((ea * 4 + bi, eb * 4 + bj), redq.at[1], fin_q.at[1, c, sub], frq.at[1, c, sub]),
    ]
    xc, jc = a // 4, a % 4
    delta = lax.rem(xc + 4 - x, 4)
    even = (delta % 2) == 0
    odd = (delta % 2) == 1
    turned = delta == 2
    near = delta // 2
    incoming = []
    for n in (0, 1):
        for k in (0, 1):
            incoming.append((even, at(lax.rem(x + near, 4), i, 2 * jc + n, k), fin_q.at[0, k, n], frq.at[0, k, n], redq.at[0]))
            incoming.append((turned, at(lax.rem(x + 3, 4), jc, 2 * i + n, k), fin_q.at[1, k, n], frq.at[1, k, n], redq.at[0]))
        incoming.append((odd, at(x, i, 2 * jc + n, near), fin_f.at[0, n], frf.at[0, n], redf))
        incoming.append((odd, at(xc, jc, 2 * i + n, 1 - near), fin_f.at[1, n], frf.at[1, n], redf))

    barrier = pltpu.get_barrier_semaphore()

    def greet(dev):
        pl.semaphore_signal(barrier, inc=1, device_id=dev, device_id_type=MESH)

    def greet_axes(d, _):
        greet((a, lax.rem(r + d, 16)))
        greet((lax.rem(a + d, 16), r))
        return 0

    lax.fori_loop(1, 16, greet_axes, 0)
    greet(at(x, 3 - y, z, c))
    for there, dev, _, _, _ in incoming:
        @pl.when(there & jnp.logical_not(is_me(dev)))
        def _():
            greet(dev)
    expect = 31
    for dev, _, _, _ in outgoing:
        expect = expect + jnp.where(is_me(dev), 0, 1)

    lane = lax.broadcasted_iota(jnp.int32, (8, 128), 1)
    ids = jnp.zeros((8, 128), jnp.int32)
    for s in range(4):
        ids = jnp.where(lane == s, t_ref[0, 0, s], ids)
    tvec[...] = ids
    pl.semaphore_wait(barrier, expect)

    def c1(d):
        return remote(c_ref.at[r], tslice.at[a], c1s.at[d - 1], c1r.at[d - 1], (lax.rem(a + d, 16), r))

    def c1_in(d):
        return remote(c_ref.at[r], tslice.at[lax.rem(a + 16 - d, 16)], c1s.at[d - 1], c1r.at[d - 1], (a, r))

    def ti(d):
        return remote(tvec, tall.at[r], tis.at[d - 1], tir.at[d - 1], (a, lax.rem(r + d, 16)))

    def ti_in(d):
        return remote(tvec, tall.at[lax.rem(r + 16 - d, 16)], tis.at[d - 1], tir.at[d - 1], (a, r))

    def start1(d, _):
        c1(d).start()
        ti(d).start()
        return 0

    lax.fori_loop(1, 16, start1, 0)
    tslice[a] = c_ref[r]
    tall[r] = ids

    def split_x(n, _):
        rows = pl.ds(pl.multiple_of(n * 128, 128), 128)
        high, low = split(xv[rows, :])
        xh[rows, :] = high
        xl[rows, :] = low
        return 0

    for n in range(4):
        load_x(n).wait()
    lax.fori_loop(0, 12, split_x, 0)

    def wait1(d, _):
        ti_in(d).wait_recv()
        return 0

    lax.fori_loop(1, 16, wait1, 0)
    to_smem = pltpu.make_async_copy(tall.at[:, 0], tsm, tsem)
    to_smem.start()
    to_smem.wait()

    def wait1c(d, _):
        c1_in(d).wait_recv()
        return 0

    lax.fori_loop(1, 16, wait1c, 0)

    def c2(d):
        return remote(picks.at[d - 1], csel.at[:, r], c2s.at[d - 1], c2r.at[d - 1], (a, lax.rem(r + d, 16)))

    def c2_in(d):
        return remote(picks.at[d - 1], csel.at[:, lax.rem(r + 16 - d, 16)], c2s.at[d - 1], c2r.at[d - 1], (a, r))

    def start2(d, _):
        who = lax.rem(r + d, 16)
        for s in range(4):
            picks[d - 1, s] = tslice[tsm[who, s]]
        c2(d).start()
        return 0

    lax.fori_loop(1, 16, start2, 0)
    for s in range(4):
        csel[s, r] = tslice[tsm[r, s]]

    def wait2(d, _):
        c2_in(d).wait_recv()
        return 0

    lax.fori_loop(1, 16, wait2, 0)
    for s in range(4):
        high, low = split(csel[s].reshape(128, 256))
        ch[s * 128:(s + 1) * 128, :] = high
        cl[s * 128:(s + 1) * 128, :] = low

    peers = [lax.rem(i + 2, 4), 3 - i, i + 1 - 2 * c]

    def swap(k):
        return remote(hb.at[k], blk.at[:, i], has.at[k], har.at[k], (a, x * 4 + peers[k]))

    def swap_in(k):
        return remote(hb.at[k], blk.at[:, peers[k]], has.at[k], har.at[k], (a, r))

    def half_of(g):
        rows = pl.ds(pl.multiple_of(g * 384, 128), 384)
        return dot3(xh[rows, :], xl[rows, :], ch[...], cl[...], NN_DIMS)

    def chunk(value, q):
        return value[(q // 2) * 128:(q // 2 + 1) * 128, (q % 2) * 128:(q % 2 + 1) * 128]

    def turn(src, slot, p):
        rows = pl.ds(pl.multiple_of(p * 128, 128), 128)
        for q in range(6):
            high, low = split(src[q, p])
            gg[slot, 0, rows, q * 128:(q + 1) * 128] = high
            gg[slot, 1, rows, q * 128:(q + 1) * 128] = low

    def turn_half(src, start, slot):
        def body(n, _):
            rows = pl.ds(pl.multiple_of(n * 128, 128), 128)
            for q in range(3):
                high, low = split(src[start + q, n])
                eh[slot, 0, rows, q * 128:(q + 1) * 128] = high
                eh[slot, 1, rows, q * 128:(q + 1) * 128] = low
            return 0
        lax.fori_loop(0, 4, body, 0)

    mine = x // 2
    others = x_to // 2

    def whole(p, k):
        return remote(blk.at[:, p], xfull.at[:, p], xs.at[k, 0], xr.at[k, 0], (a, x_to * 4 + i))

    def part_way(p, k):
        return remote(blk.at[pl.ds(3 * mine, 3), p], xhalf.at[:, p], xs.at[k, 1], xr.at[k, 1], (a, x_back * 4 + i))

    def square(n, buf, left, right):
        for jj in range(2):
            cols = slice(jj * 256, (jj + 1) * 256)
            value = dot3(buf[left, 0], buf[left, 1], buf[right, 0, cols, :], buf[right, 1, cols, :], NT_DIMS)
            for m in range(4):
                for jl in range(2):
                    for h in range(2):
                        pc[n, h, m, 2 * jj + jl] = value[
                            m * 128 + h * 64:m * 128 + (h + 1) * 64, jl * 128:(jl + 1) * 128
                        ].reshape(2, 32, 128)

    def core_swap(n):
        return remote(pc.at[n, 1 - c], cb.at[n], ccs.at[n], ccr.at[n], (a, r + 1 - 2 * c))

    def core_sum(n):
        core_swap(n).wait_recv()
        for m in range(4):
            pc[n, c, m] = pc[n, c, m] + cb[n, m]

    def fy(d, p):
        py = lax.rem(y + d, 4)
        return remote(pf.at[py, p], ryf.at[d - 1, p], fys.at[p, d - 1], fyr.at[p, d - 1], at(x, py, z, c))

    def fz(d):
        pz = lax.rem(z + d, 8)
        return remote(sf.at[pz], rzf.at[d - 1], fzs.at[d - 1], fzr.at[d - 1], at(x, y, pz, c))

    def ey(d):
        py = lax.rem(y + d, 4)
        return remote(pc.at[1, c, py], rye.at[d - 1], eys.at[d - 1], eyr.at[d - 1], at(x, py, z, c))

    def ez(d):
        pz = lax.rem(z + d, 8)
        return remote(se_.at[pz // 2, pz % 2], rze.at[d - 1], ezs.at[d - 1], ezr.at[d - 1], at(x, y, pz, c))

    def dz(d):
        pz = lax.rem(z + d, 8)
        return remote(pc.at[0, c, :, pz // 2, pz % 2], rzd.at[d - 1], dzs.at[d - 1], dzr.at[d - 1], at(x, y, pz, c))

    def dy(d):
        py = lax.rem(y + d, 4)
        return remote(sd.at[py], ryd.at[d - 1], dys.at[d - 1], dyr.at[d - 1], at(x, py, z, c))

    def deliver(n):
        dev, src, dst, sem = outgoing[n]
        return remote(src, dst, fs.at[n], sem, dev)

    def send_out(n):
        dev, src, dst, _ = outgoing[n]

        @pl.when(jnp.logical_not(is_me(dev)))
        def _():
            deliver(n).start()

        if n < 2:
            @pl.when(is_me(dev))
            def _():
                dst[...] = src[...]

    def f_piece(p, k):
        whole(p, k).wait_recv()
        turn(xfull, 1, p)
        rows = pl.ds(pl.multiple_of(p * 128, 128), 128)
        value = dot3(gg[0, 0], gg[0, 1], gg[1, 0, rows, :], gg[1, 1, rows, :], NT_DIMS)
        for m in range(4):
            pf[m, p] = value[m * 128:(m + 1) * 128].reshape(2, 64, 128)
        for d in (2, 1, 3):
            fy(d, p).start()

    for k in range(2):
        value = half_of(peers[k])
        for q in range(6):
            hb[k, q] = chunk(value, q)
        swap(k).start()
    value = half_of(i)
    for q in range(6):
        blk[q, i] = chunk(value, q)
    whole(i, 3).start()
    value = half_of(peers[2])
    for q in range(6):
        hb[2, q] = chunk(value, q)
    swap(2).start()
    turn(blk, 0, i)
    swap_in(2).wait_recv()
    whole(peers[2], 2).start()
    turn(blk, 0, peers[2])
    swap_in(0).wait_recv()
    whole(peers[0], 0).start()
    part_way(i, 3).start()
    part_way(peers[2], 2).start()
    turn(blk, 0, peers[0])
    swap_in(1).wait_recv()
    whole(peers[1], 1).start()
    part_way(peers[0], 0).start()
    part_way(peers[1], 1).start()
    turn(blk, 0, peers[1])
    f_piece(i, 3)
    f_piece(peers[2], 2)
    f_piece(peers[0], 0)
    square(0, gg, 0, 0)
    core_swap(0).start()
    f_piece(peers[1], 1)
    core_sum(0)
    for d in (4, 3, 5, 2, 6, 1, 7):
        dz(d).start()
    turn_half(xfull, 3 * others, 1 - c)
    pieces = [(i, 3), (peers[2], 2), (peers[0], 0), (peers[1], 1)]
    for p, k in pieces:
        part_way(p, k).wait_recv()
    turn_half(xhalf, 0, c)
    square(1, eh, 0, 1)
    core_swap(1).start()
    for p, k in pieces:
        for d in (1, 2, 3):
            fy(d, p).wait_recv()
        sf[pl.ds(2 * p, 2)] = pf[y, p] + ryf[0, p] + ryf[1, p] + ryf[2, p]
    for d in (4, 3, 5, 2, 6, 1, 7):
        fz(d).start()
    core_sum(1)
    for d in (2, 1, 3):
        ey(d).start()
    for d in range(1, 8):
        dz(d).wait_recv()
    total = pc[0, c, :, z // 2, z % 2]
    for d in range(7):
        total = total + rzd[d]
    sd[...] = total
    for d in (2, 1, 3):
        dy(d).start()
    for d in (1, 2, 3):
        ey(d).wait_recv()
    se_[...] = pc[1, c, y] + rye[0] + rye[1] + rye[2]
    for d in (4, 3, 5, 2, 6, 1, 7):
        ez(d).start()
    for d in range(1, 8):
        fz(d).wait_recv()
    total = sf[z]
    for d in range(7):
        total = total + rzf[d]
    redf[...] = total
    send_out(1)
    send_out(2)
    for d in (1, 2, 3):
        dy(d).wait_recv()
    redq[0] = sd[y] + ryd[0] + ryd[1] + ryd[2]
    send_out(0)
    for d in range(1, 8):
        ez(d).wait_recv()
    total = se_[z // 2, z % 2]
    for d in range(7):
        total = total + rze[d]
    redq[1] = total
    send_out(3)
    send_out(4)

    for there, dev, dst, sem, src in incoming:
        @pl.when(there & jnp.logical_not(is_me(dev)))
        def _():
            remote(src, dst, fs.at[0], sem, (a, r)).wait_recv()

    @pl.when(delta == 0)
    def _():
        out_ref[...] = fin_q[0].reshape(128, 128)

    @pl.when(turned)
    def _():
        out_ref[...] = fin_q[0].reshape(128, 128) + fin_q[1].reshape(128, 128).T

    @pl.when(odd)
    def _():
        out_ref[...] = fin_f[0].reshape(128, 128) + fin_f[1].reshape(128, 128).T

    def drain(d, _):
        c1(d).wait_send()
        ti(d).wait_send()
        c2(d).wait_send()
        return 0

    lax.fori_loop(1, 16, drain, 0)
    for k in range(3):
        swap(k).wait_send()
    for n in range(2):
        core_swap(n).wait_send()
    for p, k in pieces:
        whole(p, k).wait_send()
        part_way(p, k).wait_send()
        for d in (1, 2, 3):
            fy(d, p).wait_send()
    for d in (1, 2, 3):
        ey(d).wait_send()
        dy(d).wait_send()
    for d in range(1, 8):
        fz(d).wait_send()
        ez(d).wait_send()
        dz(d).wait_send()
    for n in range(5):
        @pl.when(jnp.logical_not(is_me(outgoing[n][0])))
        def _():
            deliver(n).wait_send()


def on_device(three_index, coefficients, tile_index):
    dma = pltpu.SemaphoreType.DMA
    vm = pltpu.VMEM
    return pl.pallas_call(
        kernel,
        out_shape=jax.ShapeDtypeStruct((128, 128), F32),
        in_specs=[
            pl.BlockSpec(memory_space=pl.ANY),
            pl.BlockSpec(memory_space=pltpu.VMEM),
            pl.BlockSpec(memory_space=pltpu.SMEM),
        ],
        out_specs=pl.BlockSpec(memory_space=pltpu.VMEM),
        scratch_shapes=[
            vm((1536, 512), F32), vm((1536, 512), BF16), vm((1536, 512), BF16),
            vm((16, 8, 256), F32), vm((8, 128), jnp.int32), vm((16, 8, 128), jnp.int32),
            pltpu.SMEM((16, 128), jnp.int32),
            vm((15, 4, 8, 256), F32), vm((4, 16, 8, 256), F32),
            vm((512, 256), BF16), vm((512, 256), BF16),
            vm((3, 6, 128, 128), F32), vm((6, 4, 128, 128), F32), vm((6, 4, 128, 128), F32), vm((3, 4, 128, 128), F32),
            vm((2, 2, 512, 768), BF16), vm((2, 2, 512, 384), BF16),
            vm((2, 2, 4, 4, 2, 32, 128), F32), vm((2, 4, 4, 2, 32, 128), F32),
            vm((4, 4, 2, 64, 128), F32), vm((3, 4, 2, 64, 128), F32), vm((8, 64, 128), F32), vm((7, 64, 128), F32),
            vm((64, 128), F32),
            vm((3, 4, 2, 32, 128), F32), vm((4, 2, 32, 128), F32), vm((7, 32, 128), F32),
            vm((7, 4, 32, 128), F32), vm((4, 32, 128), F32), vm((3, 32, 128), F32),
            vm((2, 32, 128), F32), vm((2, 2, 2, 32, 128), F32), vm((2, 2, 64, 128), F32),
            dma((4,)), dma((15,)), dma((15,)), dma((15,)), dma((15,)), dma((15,)), dma((15,)), dma,
            dma((3,)), dma((3,)), dma((4, 2)), dma((4, 2)), dma((2,)), dma((2,)),
            dma((4, 3)), dma((4, 3)), dma((7,)), dma((7,)),
            dma((3,)), dma((3,)), dma((7,)), dma((7,)), dma((3,)), dma((3,)), dma((7,)), dma((7,)),
            dma((5,)), dma((2, 2, 2)), dma((2, 2)),
        ],
        compiler_params=pltpu.CompilerParams(
            collective_id=0, has_side_effects=True, vmem_limit_bytes=56 * 2**20
        ),
    )(three_index.reshape(1536, 512), coefficients.reshape(16, 8, 256), tile_index)


def solution(mesh):
    return jax.shard_map(
        on_device,
        mesh=mesh,
        in_specs=(P("aux", "row", None), P("aux", None), P("aux", "row", None)),
        out_specs=P("row", "aux"),
        check_vma=False,
    )
```

```python
import functools

import jax
import jax.numpy as jnp
from jax import lax
from jax.experimental import pallas as pl
from jax.experimental.pallas import tpu as pltpu
from jax.sharding import PartitionSpec as P

MESH = pl.DeviceIdType.MESH
F32 = jnp.float32
BF16 = jnp.bfloat16
NT_DIMS = (((1,), (1,)), ((), ()))
NN_DIMS = (((1,), (0,)), ((), ()))


def split(value):
    high = value.astype(BF16)
    return high, (value - high.astype(F32)).astype(BF16)


def dot3(lh, ll, rh, rl, dims):
    dot = functools.partial(lax.dot_general, dimension_numbers=dims, preferred_element_type=F32)
    return dot(lh, rh) + (dot(lh, rl) + dot(ll, rh))


def kernel(
    x_ref, c_ref, t_ref, out_ref,
    xv, xh, xl, tslice, tvec, tall, tsm, picks, csel, ch, cl,
    hb, blk, xfull, xhalf, gg, eh,
    pc, cb, pf, ryf, sf, rzf, redf, rye, se_, rze, rzd, sd, ryd, redq, fin_q, fin_f,
    loads, c1s, c1r, tis, tir, c2s, c2r, tsem, has, har, xs, xr, ccs, ccr,
    fys, fyr, fzs, fzr, eys, eyr, ezs, ezr, dys, dyr, dzs, dzr, fs, frq, frf,
):
    a = lax.axis_index("aux")
    r = lax.axis_index("row")
    lo, z = a // 8, a % 8
    x, i = r // 4, r % 4
    hi, c = i // 2, i % 2
    y = hi * 2 + lo

    def at(px, py, pz, pc):
        return (py % 2) * 8 + pz, px * 4 + (py // 2) * 2 + pc

    def remote(src, dst, ss, rs, dev):
        return pltpu.make_async_remote_copy(
            src_ref=src, dst_ref=dst, send_sem=ss, recv_sem=rs, device_id=dev, device_id_type=MESH
        )

    def took(sem, ref):
        remote(ref, ref, sem, sem, (a, r)).wait_recv()

    def is_me(dev):
        return (dev[0] == a) & (dev[1] == r)

    def load_x(n):
        return pltpu.make_async_copy(x_ref.at[pl.ds(n * 384, 384)], xv.at[pl.ds(n * 384, 384)], loads)

    for n in range(4):
        load_x(n).start()

    sub = z % 2
    bi, bj = y, z // 2
    step = 2 * c - 1
    x_to = lax.rem(x + 4 + step, 4)
    x_back = lax.rem(x + 4 - step, 4)
    ea, eb = lax.rem(x + 3, 4), lax.rem(x + 1, 4)
    outgoing = [
        ((x * 4 + bj, x * 4 + bi), redq.at[0], fin_q.at[0, c, sub], frq.at[0]),
        ((x_back * 4 + bj, x * 4 + bi), redf, fin_f.at[0, sub], frf.at[0]),
        ((x * 4 + bi, x_back * 4 + bj), redf, fin_f.at[1, sub], frf.at[1]),
        ((eb * 4 + bj, ea * 4 + bi), redq.at[1], fin_q.at[0, c, sub], frq.at[0]),
        ((ea * 4 + bi, eb * 4 + bj), redq.at[1], fin_q.at[1, c, sub], frq.at[1]),
    ]
    xc = a // 4
    delta = lax.rem(xc + 4 - x, 4)
    odd = (delta % 2) == 1
    turned = delta == 2

    barrier = pltpu.get_barrier_semaphore()

    def greet(dev):
        pl.semaphore_signal(barrier, inc=1, device_id=dev, device_id_type=MESH)

    def greet_axes(d, _):
        greet((a, lax.rem(r + d, 16)))
        greet((lax.rem(a + d, 16), r))
        return 0

    lax.fori_loop(1, 16, greet_axes, 0)
    lane = lax.broadcasted_iota(jnp.int32, (8, 128), 1)
    ids = jnp.zeros((8, 128), jnp.int32)
    for s in range(4):
        ids = jnp.where(lane == s, t_ref[0, 0, s], ids)
    tvec[...] = ids
    pl.semaphore_wait(barrier, 30)

    def c1(d):
        return remote(c_ref.at[r], tslice.at[a], c1s, c1r, (lax.rem(a + d, 16), r))

    def ti(d):
        return remote(tvec, tall.at[r], tis, tir, (a, lax.rem(r + d, 16)))

    def start1(d, _):
        c1(d).start()
        ti(d).start()
        return 0

    lax.fori_loop(1, 16, start1, 0)
    tslice[a] = c_ref[r]
    tall[r] = ids

    def split_x(n, _):
        rows = pl.ds(pl.multiple_of(n * 128, 128), 128)
        high, low = split(xv[rows, :])
        xh[rows, :] = high
        xl[rows, :] = low
        return 0

    pltpu.make_async_copy(x_ref, xv, loads).wait()
    lax.fori_loop(0, 12, split_x, 0)

    took(tir, tall.at[pl.ds(0, 15)])
    to_smem = pltpu.make_async_copy(tall.at[:, 0], tsm, tsem)
    to_smem.start()
    to_smem.wait()

    took(c1r, tslice.at[pl.ds(0, 15)])

    def c2(n, d):
        return remote(picks.at[d - 1, n], csel.at[n, :, r], c2s, c2r.at[n], (a, lax.rem(r + d, 16)))

    for n in range(2):
        def start2(d, _):
            who = lax.rem(r + d, 16)
            for s in range(4):
                picks[d - 1, n, s] = tslice[tsm[who, s], :, n * 128:(n + 1) * 128]
            c2(n, d).start()
            return 0

        lax.fori_loop(1, 16, start2, 0)
    for n in range(2):
        for s in range(4):
            csel[n, s, r] = tslice[tsm[r, s], :, n * 128:(n + 1) * 128]

    def take_c(n):
        took(c2r.at[n], picks.at[:, n])
        cols = slice(n * 128, (n + 1) * 128)
        for s in range(4):
            high, low = split(csel[n, s].reshape(128, 128))
            ch[s * 128:(s + 1) * 128, cols] = high
            cl[s * 128:(s + 1) * 128, cols] = low

    peers = [lax.rem(i + 2, 4), 3 - i, i + 1 - 2 * c]

    def swap(k, n):
        return remote(hb.at[k, pl.ds(3 * n, 3)], blk.at[pl.ds(3 * n, 3), i], has, har.at[2 * k + n], (a, x * 4 + peers[k]))

    def swap_in(k, n):
        return remote(hb.at[k, pl.ds(3 * n, 3)], blk.at[pl.ds(3 * n, 3), peers[k]], has, har.at[2 * k + n], (a, r))

    def half_of(g, n):
        rows = pl.ds(pl.multiple_of(g * 384, 128), 384)
        cols = slice(n * 128, (n + 1) * 128)
        return dot3(xh[rows, :], xl[rows, :], ch[:, cols], cl[:, cols], NN_DIMS).reshape(3, 128, 128)

    def turn(src, slot, p):
        rows = pl.ds(pl.multiple_of(p * 128, 128), 128)
        for q in range(6):
            high, low = split(src[q, p])
            gg[slot, 0, rows, q * 128:(q + 1) * 128] = high
            gg[slot, 1, rows, q * 128:(q + 1) * 128] = low

    def turn_half(src, start, slot):
        def body(n, _):
            rows = pl.ds(pl.multiple_of(n * 128, 128), 128)
            for q in range(3):
                high, low = split(src[start + q, n])
                eh[slot, 0, rows, q * 128:(q + 1) * 128] = high
                eh[slot, 1, rows, q * 128:(q + 1) * 128] = low
            return 0
        lax.fori_loop(0, 4, body, 0)

    mine = x // 2
    others = x_to // 2

    def whole(p, k, n):
        part = pl.ds(3 * n, 3)
        return remote(blk.at[part, p], xfull.at[part, p], xs.at[0], xr.at[2 * k + n], (a, x_to * 4 + i))

    def part_way(p):
        return remote(blk.at[pl.ds(3 * mine, 3), p], xhalf.at[:, p], xs.at[1], xr.at[8], (a, x_back * 4 + i))

    def get_whole(p, k):
        for n in range(2):
            whole(p, k, n).wait_recv()
        turn(xfull, 1, p)

    def square(n, buf, left, right):
        for jj in range(2):
            cols = slice(jj * 256, (jj + 1) * 256)
            value = dot3(buf[left, 0], buf[left, 1], buf[right, 0, cols, :], buf[right, 1, cols, :], NT_DIMS)
            for m in range(4):
                for jl in range(2):
                    for h in range(2):
                        pc[n, h, m, 2 * jj + jl] = value[
                            m * 128 + h * 64:m * 128 + (h + 1) * 64, jl * 128:(jl + 1) * 128
                        ].reshape(2, 32, 128)

    def core_swap(n):
        return remote(pc.at[n, 1 - c], cb.at[n], ccs, ccr.at[n], (a, r + 1 - 2 * c))

    def core_sum(n):
        core_swap(n).wait_recv()
        for m in range(4):
            pc[n, c, m] = pc[n, c, m] + cb[n, m]

    def fy(d, p):
        py = lax.rem(y + d, 4)
        return remote(pf.at[py, p], ryf.at[d - 1, p], fys, fyr, at(x, py, z, c))

    def fz(d):
        pz = lax.rem(z + d, 8)
        return remote(sf.at[pz], rzf.at[d - 1], fzs, fzr, at(x, y, pz, c))

    def ey(d):
        py = lax.rem(y + d, 4)
        return remote(pc.at[1, c, py], rye.at[d - 1], eys, eyr, at(x, py, z, c))

    def ez(d):
        pz = lax.rem(z + d, 8)
        return remote(se_.at[pz // 2, pz % 2], rze.at[d - 1], ezs, ezr, at(x, y, pz, c))

    def d_own(pz):
        return pc.at[0, c, :, pz // 2, pz % 2]

    def dz(d):
        pz = lax.rem(z + d, 8)
        return remote(d_own(pz), rzd.at[d - 1], dzs, dzr, at(x, y, pz, c))

    def dy(d):
        py = lax.rem(y + d, 4)
        return remote(sd.at[py], ryd.at[d - 1], dys, dyr, at(x, py, z, c))

    def deliver(n):
        dev, src, dst, sem = outgoing[n]
        return remote(src, dst, fs.at[n], sem, dev)

    def send_out(n):
        dev, src, dst, _ = outgoing[n]

        @pl.when(jnp.logical_not(is_me(dev)))
        def _():
            deliver(n).start()

        if n < 2:
            @pl.when(is_me(dev))
            def _():
                pltpu.make_async_copy(src, dst, outgoing[n][3]).start()

    def f_piece(p, k):
        get_whole(p, k)
        rows = pl.ds(pl.multiple_of(p * 128, 128), 128)
        value = dot3(gg[0, 0], gg[0, 1], gg[1, 0, rows, :], gg[1, 1, rows, :], NT_DIMS)
        for m in range(4):
            pf[m, p] = value[m * 128:(m + 1) * 128].reshape(2, 64, 128)
        for d in (2, 1, 3):
            fy(d, p).start()

    pair = hi * 2

    def f_row(m):
        rows = pl.ds(pl.multiple_of(m * 128, 128), 128)
        cols = pl.ds(pl.multiple_of(pair * 128, 256), 256)
        value = dot3(gg[0, 0, rows, :], gg[0, 1, rows, :], gg[1, 0, cols, :], gg[1, 1, cols, :], NT_DIMS)
        for n in range(2):
            pf[m, pair + n] = value[:, n * 128:(n + 1) * 128].reshape(2, 64, 128)
        d = lax.rem(m + 4 - y, 4)

        @pl.when(d > 0)
        def _():
            for n in range(2):
                fy(d, pair + n).start()

    def half_out(k, n):
        hb[k, 3 * n:3 * n + 3] = half_of(peers[k], n)
        swap(k, n).start()

    def half_own(n):
        blk[3 * n:3 * n + 3, i] = half_of(i, n)
        whole(i, 3, n).start()

    def arrived(k, n):
        swap_in(k, n).wait_recv()
        whole(peers[k], k, n).start()

    take_c(0)
    half_out(0, 0)
    half_own(0)
    half_out(2, 0)
    half_out(1, 0)
    take_c(1)
    half_out(0, 1)
    half_own(1)
    arrived(2, 0)
    half_out(2, 1)
    half_out(1, 1)
    turn(blk, 0, i)
    arrived(2, 1)
    turn(blk, 0, peers[2])
    arrived(0, 0)
    get_whole(i, 3)
    get_whole(peers[2], 2)
    part_way(i).start()
    part_way(peers[2]).start()
    f_row(i)
    f_row(peers[2])
    arrived(1, 0)
    arrived(0, 1)
    turn(blk, 0, peers[0])
    part_way(peers[0]).start()
    f_row(peers[0])
    arrived(1, 1)
    turn(blk, 0, peers[1])
    part_way(peers[1]).start()
    square(0, gg, 0, 0)
    core_swap(0).start()
    f_row(peers[1])
    core_sum(0)
    for d in (4, 3, 5, 2, 6, 1, 7):
        dz(d).start()
    f_piece(peers[0], 0)
    f_piece(peers[1], 1)
    turn_half(xfull, 3 * others, 1 - c)
    took(xr.at[8], xhalf)
    turn_half(xhalf, 0, c)
    square(1, eh, 0, 1)
    core_swap(1).start()
    core_sum(1)
    for d in (2, 1, 3):
        ey(d).start()
    took(fyr, ryf)
    for m in range(4):
        sf[2 * m:2 * m + 2] = pf[y, m] + ryf[0, m] + ryf[1, m] + ryf[2, m]
    for d in (4, 3, 5, 2, 6, 1, 7):
        fz(d).start()
    took(eyr, rye)
    se_[...] = pc[1, c, y] + rye[0] + rye[1] + rye[2]
    for d in (4, 3, 5, 2, 6, 1, 7):
        ez(d).start()
    took(dzr, rzd)
    total = d_own(z)[...]
    for d in range(7):
        total = total + rzd[d]
    sd[...] = total
    for d in (2, 1, 3):
        dy(d).start()
    took(fzr, rzf)
    total = sf[z]
    for d in range(7):
        total = total + rzf[d]
    redf[...] = total
    send_out(1)
    send_out(2)
    took(dyr, ryd)
    redq[0] = sd[y] + ryd[0] + ryd[1] + ryd[2]
    send_out(0)
    took(ezr, rze)
    total = se_[z // 2, z % 2]
    for d in range(7):
        total = total + rze[d]
    redq[1] = total
    send_out(3)
    send_out(4)

    @pl.when(delta == 0)
    def _():
        took(frq.at[0], fin_q.at[0])
        out_ref[...] = fin_q[0].reshape(128, 128)

    @pl.when(turned)
    def _():
        took(frq.at[0], fin_q.at[0])
        took(frq.at[1], fin_q.at[1])
        out_ref[...] = fin_q[0].reshape(128, 128) + fin_q[1].reshape(128, 128).T

    @pl.when(odd)
    def _():
        took(frf.at[0], fin_f.at[0])
        took(frf.at[1], fin_f.at[1])
        out_ref[...] = fin_f[0].reshape(128, 128) + fin_f[1].reshape(128, 128).T

    for sem, ref in (
        (c1s, tslice.at[pl.ds(0, 15)]), (tis, tall.at[pl.ds(0, 15)]), (c2s, picks), (has, hb),
        (xs.at[0], blk), (xs.at[1], xhalf), (ccs, cb), (fys, ryf), (fzs, rzf), (eys, rye), (ezs, rze), (dzs, rzd), (dys, ryd),
    ):
        took(sem, ref)
    for n in range(5):
        @pl.when(jnp.logical_not(is_me(outgoing[n][0])))
        def _():
            deliver(n).wait_send()


def on_device(three_index, coefficients, tile_index):
    dma = pltpu.SemaphoreType.DMA
    vm = pltpu.VMEM
    return pl.pallas_call(
        kernel,
        out_shape=jax.ShapeDtypeStruct((128, 128), F32),
        in_specs=[
            pl.BlockSpec(memory_space=pl.ANY),
            pl.BlockSpec(memory_space=pltpu.VMEM),
            pl.BlockSpec(memory_space=pltpu.SMEM),
        ],
        out_specs=pl.BlockSpec(memory_space=pltpu.VMEM),
        scratch_shapes=[
            vm((1536, 512), F32), vm((1536, 512), BF16), vm((1536, 512), BF16),
            vm((16, 8, 256), F32), vm((8, 128), jnp.int32), vm((16, 8, 128), jnp.int32),
            pltpu.SMEM((16, 128), jnp.int32),
            vm((15, 2, 4, 8, 128), F32), vm((2, 4, 16, 8, 128), F32),
            vm((512, 256), BF16), vm((512, 256), BF16),
            vm((3, 6, 128, 128), F32), vm((6, 4, 128, 128), F32), vm((6, 4, 128, 128), F32), vm((3, 4, 128, 128), F32),
            vm((2, 2, 512, 768), BF16), vm((2, 2, 512, 384), BF16),
            vm((2, 2, 4, 4, 2, 32, 128), F32), vm((2, 4, 4, 2, 32, 128), F32),
            vm((4, 4, 2, 64, 128), F32), vm((3, 4, 2, 64, 128), F32), vm((8, 64, 128), F32), vm((7, 64, 128), F32),
            vm((64, 128), F32),
            vm((3, 4, 2, 32, 128), F32), vm((4, 2, 32, 128), F32), vm((7, 32, 128), F32),
            vm((7, 4, 32, 128), F32), vm((4, 32, 128), F32), vm((3, 32, 128), F32),
            vm((2, 32, 128), F32), vm((2, 2, 2, 32, 128), F32), vm((2, 2, 64, 128), F32),
            dma, dma, dma, dma, dma, dma, dma((2,)), dma,
            dma, dma((6,)), dma((2,)), dma((9,)), dma, dma((2,)),
            dma, dma, dma, dma, dma, dma, dma, dma, dma, dma, dma, dma,
            dma((5,)), dma((2,)), dma((2,)),
        ],
        compiler_params=pltpu.CompilerParams(
            collective_id=0, has_side_effects=True, vmem_limit_bytes=56 * 2**20
        ),
    )(three_index.reshape(1536, 512), coefficients.reshape(16, 8, 256), tile_index)


def solution(mesh):
    return jax.shard_map(
        on_device,
        mesh=mesh,
        in_specs=(P("aux", "row", None), P("aux", None), P("aux", "row", None)),
        out_specs=P("row", "aux"),
        check_vma=False,
    )
```

```python
import functools

import jax
import jax.numpy as jnp
from jax import lax
from jax.experimental import pallas as pl
from jax.experimental.pallas import tpu as pltpu
from jax.sharding import PartitionSpec as P

MESH = pl.DeviceIdType.MESH
F32 = jnp.float32
BF16 = jnp.bfloat16
NT_DIMS = (((1,), (1,)), ((), ()))
NN_DIMS = (((1,), (0,)), ((), ()))


def split(value):
    high = value.astype(BF16)
    return high, (value - high.astype(F32)).astype(BF16)


def dot3(lh, ll, rh, rl, dims):
    dot = functools.partial(lax.dot_general, dimension_numbers=dims, preferred_element_type=F32)
    return dot(lh, rh) + (dot(lh, rl) + dot(ll, rh))


def kernel(
    x_ref, c_ref, t_ref, out_ref,
    xv, xh, xl, tslice, tvec, tall, tsm, tloc, picks, csel, ch, cl,
    hb, blk, xfull, xhalf, gg, eh,
    pc, cb, pf, ryf, sf, rzf, redf, rye, se_, rze, rzd, sd, ryd, redq, fin_q, fin_f,
    loads, c1s, c1r, tis, tir, c2s, c2r, tsem, has, har, xs, xr, ccs, ccr,
    fys, fyr, fzs, fzr, eys, eyr, ezs, ezr, dys, dyr, dzs, dzr, fs, frq, frf,
):
    a = lax.axis_index("aux")
    r = lax.axis_index("row")
    lo, z = a // 8, a % 8
    x, i = r // 4, r % 4
    hi, c = i // 2, i % 2
    y = hi * 2 + lo

    def at(px, py, pz, pc):
        return (py % 2) * 8 + pz, px * 4 + (py // 2) * 2 + pc

    def remote(src, dst, ss, rs, dev):
        return pltpu.make_async_remote_copy(
            src_ref=src, dst_ref=dst, send_sem=ss, recv_sem=rs, device_id=dev, device_id_type=MESH
        )

    def took(sem, ref):
        remote(ref, ref, sem, sem, (a, r)).wait_recv()

    def is_me(dev):
        return (dev[0] == a) & (dev[1] == r)

    barrier = pltpu.get_barrier_semaphore()

    def greet(dev):
        pl.semaphore_signal(barrier, inc=1, device_id=dev, device_id_type=MESH)

    def greet_axes(d, _):
        greet((a, lax.rem(r + d, 16)))
        greet((lax.rem(a + d, 16), r))
        return 0

    lax.fori_loop(1, 16, greet_axes, 0)
    own_c = pltpu.make_async_copy(c_ref.at[r], tslice.at[a], loads.at[1])
    own_t = pltpu.make_async_copy(t_ref.at[0], tloc, loads.at[2])
    own_t.start()
    own_c.start()

    def load_x(n):
        return pltpu.make_async_copy(x_ref.at[pl.ds(n * 384, 384)], xv.at[pl.ds(n * 384, 384)], loads.at[0])

    for n in range(4):
        load_x(n).start()

    sub = z % 2
    bi, bj = y, z // 2
    step = 2 * c - 1
    x_to = lax.rem(x + 4 + step, 4)
    x_back = lax.rem(x + 4 - step, 4)
    ea, eb = lax.rem(x + 3, 4), lax.rem(x + 1, 4)
    outgoing = [
        ((x * 4 + bj, x * 4 + bi), redq.at[0], fin_q.at[0, c, sub], frq.at[0]),
        ((x_back * 4 + bj, x * 4 + bi), redf, fin_f.at[0, sub], frf.at[0]),
        ((x * 4 + bi, x_back * 4 + bj), redf, fin_f.at[1, sub], frf.at[1]),
        ((eb * 4 + bj, ea * 4 + bi), redq.at[1], fin_q.at[0, c, sub], frq.at[0]),
        ((ea * 4 + bi, eb * 4 + bj), redq.at[1], fin_q.at[1, c, sub], frq.at[1]),
    ]
    xc = a // 4
    delta = lax.rem(xc + 4 - x, 4)
    odd = (delta % 2) == 1
    turned = delta == 2

    lane = lax.broadcasted_iota(jnp.int32, (8, 128), 1)
    own_t.wait()
    ids = jnp.zeros((8, 128), jnp.int32)
    for s in range(4):
        ids = jnp.where(lane == s, tloc[0, s], ids)
    tvec[...] = ids
    own_c.wait()
    pl.semaphore_wait(barrier, 30)

    def c1(d):
        return remote(tslice.at[a], tslice.at[a], c1s, c1r, (lax.rem(a + d, 16), r))

    def ti(d):
        return remote(tvec, tall.at[r], tis, tir, (a, lax.rem(r + d, 16)))

    def start1(d, _):
        c1(d).start()
        ti(d).start()
        return 0

    lax.fori_loop(1, 16, start1, 0)
    tall[r] = ids

    def split_x(n, _):
        rows = pl.ds(pl.multiple_of(n * 128, 128), 128)
        high, low = split(xv[rows, :])
        xh[rows, :] = high
        xl[rows, :] = low
        return 0

    pltpu.make_async_copy(x_ref, xv, loads.at[0]).wait()
    lax.fori_loop(0, 12, split_x, 0)

    took(tir, tall.at[pl.ds(0, 15)])
    to_smem = pltpu.make_async_copy(tall.at[:, 0], tsm, tsem)
    to_smem.start()
    to_smem.wait()

    took(c1r, tslice.at[pl.ds(0, 15)])

    def c2(n, d):
        return remote(picks.at[d - 1, n], csel.at[n, :, r], c2s, c2r.at[n], (a, lax.rem(r + d, 16)))

    for n in range(2):
        def start2(d, _):
            who = lax.rem(r + d, 16)
            for s in range(4):
                picks[d - 1, n, s] = tslice[tsm[who, s], :, n * 128:(n + 1) * 128]
            c2(n, d).start()
            return 0

        lax.fori_loop(1, 16, start2, 0)
    for n in range(2):
        for s in range(4):
            csel[n, s, r] = tslice[tsm[r, s], :, n * 128:(n + 1) * 128]

    def take_c(n):
        took(c2r.at[n], picks.at[:, n])
        cols = slice(n * 128, (n + 1) * 128)
        for s in range(4):
            high, low = split(csel[n, s].reshape(128, 128))
            ch[s * 128:(s + 1) * 128, cols] = high
            cl[s * 128:(s + 1) * 128, cols] = low

    peers = [lax.rem(i + 2, 4), 3 - i, i + 1 - 2 * c]

    def swap(k, n):
        return remote(hb.at[k, pl.ds(3 * n, 3)], blk.at[pl.ds(3 * n, 3), i], has, har.at[2 * k + n], (a, x * 4 + peers[k]))

    def swap_in(k, n):
        return remote(hb.at[k, pl.ds(3 * n, 3)], blk.at[pl.ds(3 * n, 3), peers[k]], has, har.at[2 * k + n], (a, r))

    def half_of(g, n):
        rows = pl.ds(pl.multiple_of(g * 384, 128), 384)
        cols = slice(n * 128, (n + 1) * 128)
        return dot3(xh[rows, :], xl[rows, :], ch[:, cols], cl[:, cols], NN_DIMS).reshape(3, 128, 128)

    def turn(src, slot, p):
        rows = pl.ds(pl.multiple_of(p * 128, 128), 128)
        for q in range(6):
            high, low = split(src[q, p])
            gg[slot, 0, rows, q * 128:(q + 1) * 128] = high
            gg[slot, 1, rows, q * 128:(q + 1) * 128] = low

    def turn_half(src, start, slot):
        def body(n, _):
            rows = pl.ds(pl.multiple_of(n * 128, 128), 128)
            for q in range(3):
                high, low = split(src[start + q, n])
                eh[slot, 0, rows, q * 128:(q + 1) * 128] = high
                eh[slot, 1, rows, q * 128:(q + 1) * 128] = low
            return 0
        lax.fori_loop(0, 4, body, 0)

    mine = x // 2
    others = x_to // 2

    def whole(p, k, n):
        part = pl.ds(3 * n, 3)
        return remote(blk.at[part, p], xfull.at[part, p], xs.at[0], xr.at[2 * k + n], (a, x_to * 4 + i))

    def part_way(p):
        return remote(blk.at[pl.ds(3 * mine, 3), p], xhalf.at[:, p], xs.at[1], xr.at[8], (a, x_back * 4 + i))

    def get_whole(p, k):
        for n in range(2):
            whole(p, k, n).wait_recv()
        turn(xfull, 1, p)

    def square(n, buf, left, right):
        for jj in range(2):
            cols = slice(jj * 256, (jj + 1) * 256)
            value = dot3(buf[left, 0], buf[left, 1], buf[right, 0, cols, :], buf[right, 1, cols, :], NT_DIMS)
            for m in range(4):
                for jl in range(2):
                    for h in range(2):
                        pc[n, h, m, 2 * jj + jl] = value[
                            m * 128 + h * 64:m * 128 + (h + 1) * 64, jl * 128:(jl + 1) * 128
                        ].reshape(2, 32, 128)

    def core_swap(n):
        return remote(pc.at[n, 1 - c], cb.at[n], ccs, ccr.at[n], (a, r + 1 - 2 * c))

    def core_sum(n):
        core_swap(n).wait_recv()
        for m in range(4):
            pc[n, c, m] = pc[n, c, m] + cb[n, m]

    def fy(d, p):
        py = lax.rem(y + d, 4)
        return remote(pf.at[py, p], ryf.at[d - 1, p], fys, fyr, at(x, py, z, c))

    def fz(d):
        pz = lax.rem(z + d, 8)
        return remote(sf.at[pz], rzf.at[d - 1], fzs, fzr, at(x, y, pz, c))

    def ey(d):
        py = lax.rem(y + d, 4)
        return remote(pc.at[1, c, py], rye.at[d - 1], eys, eyr, at(x, py, z, c))

    def ez(d):
        pz = lax.rem(z + d, 8)
        return remote(se_.at[pz // 2, pz % 2], rze.at[d - 1], ezs, ezr, at(x, y, pz, c))

    def d_own(pz):
        return pc.at[0, c, :, pz // 2, pz % 2]

    def dz(d):
        pz = lax.rem(z + d, 8)
        return remote(d_own(pz), rzd.at[d - 1], dzs, dzr, at(x, y, pz, c))

    def dy(d):
        py = lax.rem(y + d, 4)
        return remote(sd.at[py], ryd.at[d - 1], dys, dyr, at(x, py, z, c))

    def deliver(n):
        dev, src, dst, sem = outgoing[n]
        return remote(src, dst, fs.at[n], sem, dev)

    def send_out(n):
        dev, src, dst, _ = outgoing[n]

        @pl.when(jnp.logical_not(is_me(dev)))
        def _():
            deliver(n).start()

        if n < 2:
            @pl.when(is_me(dev))
            def _():
                pltpu.make_async_copy(src, dst, outgoing[n][3]).start()

    def f_piece(p, k):
        get_whole(p, k)
        rows = pl.ds(pl.multiple_of(p * 128, 128), 128)
        value = dot3(gg[0, 0], gg[0, 1], gg[1, 0, rows, :], gg[1, 1, rows, :], NT_DIMS)
        for m in range(4):
            pf[m, p] = value[m * 128:(m + 1) * 128].reshape(2, 64, 128)
        for d in (2, 1, 3):
            fy(d, p).start()

    pair = hi * 2

    def f_row(m):
        rows = pl.ds(pl.multiple_of(m * 128, 128), 128)
        cols = pl.ds(pl.multiple_of(pair * 128, 256), 256)
        value = dot3(gg[0, 0, rows, :], gg[0, 1, rows, :], gg[1, 0, cols, :], gg[1, 1, cols, :], NT_DIMS)
        for n in range(2):
            pf[m, pair + n] = value[:, n * 128:(n + 1) * 128].reshape(2, 64, 128)
        d = lax.rem(m + 4 - y, 4)

        @pl.when(d > 0)
        def _():
            for n in range(2):
                fy(d, pair + n).start()

    def half_out(k, n):
        hb[k, 3 * n:3 * n + 3] = half_of(peers[k], n)
        swap(k, n).start()

    def half_own(n):
        blk[3 * n:3 * n + 3, i] = half_of(i, n)
        whole(i, 3, n).start()

    def arrived(k, n):
        swap_in(k, n).wait_recv()
        whole(peers[k], k, n).start()

    take_c(0)
    half_out(0, 0)
    half_own(0)
    half_out(2, 0)
    half_out(1, 0)
    take_c(1)
    half_out(0, 1)
    half_own(1)
    arrived(2, 0)
    half_out(2, 1)
    half_out(1, 1)
    turn(blk, 0, i)
    arrived(2, 1)
    turn(blk, 0, peers[2])
    arrived(0, 0)
    get_whole(i, 3)
    get_whole(peers[2], 2)
    part_way(i).start()
    part_way(peers[2]).start()
    f_row(i)
    f_row(peers[2])
    arrived(1, 0)
    arrived(0, 1)
    turn(blk, 0, peers[0])
    part_way(peers[0]).start()
    f_row(peers[0])
    arrived(1, 1)
    turn(blk, 0, peers[1])
    part_way(peers[1]).start()
    square(0, gg, 0, 0)
    core_swap(0).start()
    f_row(peers[1])
    core_sum(0)
    for d in (4, 3, 5, 2, 6, 1, 7):
        dz(d).start()
    f_piece(peers[0], 0)
    f_piece(peers[1], 1)
    turn_half(xfull, 3 * others, 1 - c)
    took(xr.at[8], xhalf)
    turn_half(xhalf, 0, c)
    square(1, eh, 0, 1)
    core_swap(1).start()
    core_sum(1)
    for d in (2, 1, 3):
        ey(d).start()
    took(fyr, ryf)
    for m in range(4):
        sf[2 * m:2 * m + 2] = pf[y, m] + ryf[0, m] + ryf[1, m] + ryf[2, m]
    for d in (4, 3, 5, 2, 6, 1, 7):
        fz(d).start()
    took(eyr, rye)
    se_[...] = pc[1, c, y] + rye[0] + rye[1] + rye[2]
    for d in (4, 3, 5, 2, 6, 1, 7):
        ez(d).start()
    took(dzr, rzd)
    total = d_own(z)[...]
    for d in range(7):
        total = total + rzd[d]
    sd[...] = total
    for d in (2, 1, 3):
        dy(d).start()
    took(fzr, rzf)
    total = sf[z]
    for d in range(7):
        total = total + rzf[d]
    redf[...] = total
    send_out(1)
    send_out(2)
    took(dyr, ryd)
    redq[0] = sd[y] + ryd[0] + ryd[1] + ryd[2]
    send_out(0)
    took(ezr, rze)
    total = se_[z // 2, z % 2]
    for d in range(7):
        total = total + rze[d]
    redq[1] = total
    send_out(3)
    send_out(4)

    @pl.when(delta == 0)
    def _():
        took(frq.at[0], fin_q.at[0])
        out_ref[...] = fin_q[0].reshape(128, 128)

    @pl.when(turned)
    def _():
        took(frq.at[0], fin_q.at[0])
        took(frq.at[1], fin_q.at[1])
        out_ref[...] = fin_q[0].reshape(128, 128) + fin_q[1].reshape(128, 128).T

    @pl.when(odd)
    def _():
        took(frf.at[0], fin_f.at[0])
        took(frf.at[1], fin_f.at[1])
        out_ref[...] = fin_f[0].reshape(128, 128) + fin_f[1].reshape(128, 128).T

    for sem, ref in (
        (c1s, tslice.at[pl.ds(0, 15)]), (tis, tall.at[pl.ds(0, 15)]), (c2s, picks), (has, hb),
        (xs.at[0], blk), (xs.at[1], xhalf), (ccs, cb), (fys, ryf), (fzs, rzf), (eys, rye), (ezs, rze), (dzs, rzd), (dys, ryd),
    ):
        took(sem, ref)
    for n in range(5):
        @pl.when(jnp.logical_not(is_me(outgoing[n][0])))
        def _():
            deliver(n).wait_send()


def on_device(three_index, coefficients, tile_index):
    dma = pltpu.SemaphoreType.DMA
    vm = pltpu.VMEM
    return pl.pallas_call(
        kernel,
        out_shape=jax.ShapeDtypeStruct((128, 128), F32),
        in_specs=[
            pl.BlockSpec(memory_space=pl.ANY),
            pl.BlockSpec(memory_space=pl.ANY),
            pl.BlockSpec(memory_space=pl.ANY),
        ],
        out_specs=pl.BlockSpec(memory_space=pltpu.VMEM),
        scratch_shapes=[
            vm((1536, 512), F32), vm((1536, 512), BF16), vm((1536, 512), BF16),
            vm((16, 8, 256), F32), vm((8, 128), jnp.int32), vm((16, 8, 128), jnp.int32),
            pltpu.SMEM((16, 128), jnp.int32), pltpu.SMEM((1, 4), jnp.int32),
            vm((15, 2, 4, 8, 128), F32), vm((2, 4, 16, 8, 128), F32),
            vm((512, 256), BF16), vm((512, 256), BF16),
            vm((3, 6, 128, 128), F32), vm((6, 4, 128, 128), F32), vm((6, 4, 128, 128), F32), vm((3, 4, 128, 128), F32),
            vm((2, 2, 512, 768), BF16), vm((2, 2, 512, 384), BF16),
            vm((2, 2, 4, 4, 2, 32, 128), F32), vm((2, 4, 4, 2, 32, 128), F32),
            vm((4, 4, 2, 64, 128), F32), vm((3, 4, 2, 64, 128), F32), vm((8, 64, 128), F32), vm((7, 64, 128), F32),
            vm((64, 128), F32),
            vm((3, 4, 2, 32, 128), F32), vm((4, 2, 32, 128), F32), vm((7, 32, 128), F32),
            vm((7, 4, 32, 128), F32), vm((4, 32, 128), F32), vm((3, 32, 128), F32),
            vm((2, 32, 128), F32), vm((2, 2, 2, 32, 128), F32), vm((2, 2, 64, 128), F32),
            dma((3,)), dma, dma, dma, dma, dma, dma((2,)), dma,
            dma, dma((6,)), dma((2,)), dma((9,)), dma, dma((2,)),
            dma, dma, dma, dma, dma, dma, dma, dma, dma, dma, dma, dma,
            dma((5,)), dma((2,)), dma((2,)),
        ],
        compiler_params=pltpu.CompilerParams(
            collective_id=0, has_side_effects=True, vmem_limit_bytes=56 * 2**20
        ),
    )(three_index.reshape(1536, 512), coefficients.reshape(16, 8, 256), tile_index)


def solution(mesh):
    return jax.shard_map(
        on_device,
        mesh=mesh,
        in_specs=(P("aux", "row", None), P("aux", None), P("aux", "row", None)),
        out_specs=P("row", "aux"),
        check_vma=False,
    )
```

```python
import functools

import jax
import jax.numpy as jnp
from jax import lax
from jax.experimental import pallas as pl
from jax.experimental.pallas import tpu as pltpu
from jax.sharding import PartitionSpec as P

MESH = pl.DeviceIdType.MESH
F32 = jnp.float32
BF16 = jnp.bfloat16
NT_DIMS = (((1,), (1,)), ((), ()))
NN_DIMS = (((1,), (0,)), ((), ()))


def split(value):
    high = value.astype(BF16)
    return high, (value - high.astype(F32)).astype(BF16)


def dot3(lh, ll, rh, rl, dims):
    dot = functools.partial(lax.dot_general, dimension_numbers=dims, preferred_element_type=F32)
    return dot(lh, rh) + (dot(lh, rl) + dot(ll, rh))


def kernel(
    x_ref, c_ref, t_ref, out_ref,
    xv, xh, xl, tslice, tvec, tall, tsm, tloc, picks, csel, ch, cl,
    hb, blk, xfull, xhalf, gg, eh,
    pc, cb, pf, ryf, sf, rzf, redf, rye, se_, rze, rzd, sd, ryd, redq, fin_q, fin_f,
    loads, c1s, c1r, tis, tir, c2s, c2r, tsem, has, har, xs, xr, ccs, ccr,
    fys, fyr, fzs, fzr, eys, eyr, ezs, ezr, dys, dyr, dzs, dzr, fs, frq, frf,
):
    a = lax.axis_index("aux")
    r = lax.axis_index("row")
    lo, z = a // 8, a % 8
    x, i = r // 4, r % 4
    hi, c = i // 2, i % 2
    y = hi * 2 + lo

    def at(px, py, pz, pc):
        return (py % 2) * 8 + pz, px * 4 + (py // 2) * 2 + pc

    def remote(src, dst, ss, rs, dev):
        return pltpu.make_async_remote_copy(
            src_ref=src, dst_ref=dst, send_sem=ss, recv_sem=rs, device_id=dev, device_id_type=MESH
        )

    def took(sem, ref):
        remote(ref, ref, sem, sem, (a, r)).wait_recv()

    def is_me(dev):
        return (dev[0] == a) & (dev[1] == r)

    barrier = pltpu.get_barrier_semaphore()

    def greet(dev):
        pl.semaphore_signal(barrier, inc=1, device_id=dev, device_id_type=MESH)

    def greet_axes(d, _):
        greet((a, lax.rem(r + d, 16)))
        greet((lax.rem(a + d, 16), r))
        return 0

    lax.fori_loop(1, 16, greet_axes, 0)
    own_c = pltpu.make_async_copy(c_ref.at[r], tslice.at[a], loads.at[1])
    own_t = pltpu.make_async_copy(t_ref.at[0], tloc, loads.at[2])
    own_t.start()
    own_c.start()

    def load_x(n):
        return pltpu.make_async_copy(x_ref.at[pl.ds(n * 384, 384)], xv.at[pl.ds(n * 384, 384)], loads.at[0])

    for n in range(4):
        load_x(n).start()

    def owned(pz, side):
        far = jnp.where(pz // 4 == side, 0, 1)
        return jnp.where(far == 0, pz % 4, 3 - pz % 4), far

    side = (x + 1) % 2
    bi = y
    bj, sub = owned(z, side)
    dj, dsub = owned(z, 1 - side)
    step = 2 * c - 1
    x_to = lax.rem(x + 4 + step, 4)
    x_back = lax.rem(x + 4 - step, 4)
    ea, eb = lax.rem(x + 3, 4), lax.rem(x + 1, 4)
    outgoing = [
        ((x * 4 + dj, x * 4 + bi), redq.at[0], fin_q.at[0, c, dsub], frq.at[0]),
        ((x_back * 4 + bj, x * 4 + bi), redf, fin_f.at[0, sub], frf.at[0]),
        ((x * 4 + bi, x_back * 4 + bj), redf, fin_f.at[1, sub], frf.at[1]),
        ((eb * 4 + bj, ea * 4 + bi), redq.at[1], fin_q.at[0, c, sub], frq.at[0]),
        ((ea * 4 + bi, eb * 4 + bj), redq.at[1], fin_q.at[1, c, sub], frq.at[1]),
    ]
    xc = a // 4
    delta = lax.rem(xc + 4 - x, 4)
    odd = (delta % 2) == 1
    turned = delta == 2

    lane = lax.broadcasted_iota(jnp.int32, (8, 128), 1)
    own_t.wait()
    ids = jnp.zeros((8, 128), jnp.int32)
    for s in range(4):
        ids = jnp.where(lane == s, tloc[0, s], ids)
    tvec[...] = ids
    own_c.wait()
    pl.semaphore_wait(barrier, 30)

    def c1(d):
        return remote(tslice.at[a], tslice.at[a], c1s, c1r, (lax.rem(a + d, 16), r))

    def ti(d):
        return remote(tvec, tall.at[r], tis, tir, (a, lax.rem(r + d, 16)))

    def start1(d, _):
        c1(d).start()
        ti(d).start()
        return 0

    lax.fori_loop(1, 16, start1, 0)
    tall[r] = ids

    def split_x(n, _):
        rows = pl.ds(pl.multiple_of(n * 128, 128), 128)
        high, low = split(xv[rows, :])
        xh[rows, :] = high
        xl[rows, :] = low
        return 0

    pltpu.make_async_copy(x_ref, xv, loads.at[0]).wait()
    lax.fori_loop(0, 12, split_x, 0)

    took(tir, tall.at[pl.ds(0, 15)])
    to_smem = pltpu.make_async_copy(tall.at[:, 0], tsm, tsem)
    to_smem.start()
    to_smem.wait()

    took(c1r, tslice.at[pl.ds(0, 15)])

    def c2(n, d):
        return remote(picks.at[d - 1, n], csel.at[n, :, r], c2s, c2r.at[n], (a, lax.rem(r + d, 16)))

    for n in range(2):
        def start2(d, _):
            who = lax.rem(r + d, 16)
            for s in range(4):
                picks[d - 1, n, s] = tslice[tsm[who, s], :, n * 128:(n + 1) * 128]
            c2(n, d).start()
            return 0

        lax.fori_loop(1, 16, start2, 0)
    for n in range(2):
        for s in range(4):
            csel[n, s, r] = tslice[tsm[r, s], :, n * 128:(n + 1) * 128]

    def take_c(n):
        took(c2r.at[n], picks.at[:, n])
        cols = slice(n * 128, (n + 1) * 128)
        for s in range(4):
            high, low = split(csel[n, s].reshape(128, 128))
            ch[s * 128:(s + 1) * 128, cols] = high
            cl[s * 128:(s + 1) * 128, cols] = low

    peers = [lax.rem(i + 2, 4), 3 - i, i + 1 - 2 * c]

    def swap(k, n):
        return remote(hb.at[k, pl.ds(3 * n, 3)], blk.at[pl.ds(3 * n, 3), i], has, har.at[2 * k + n], (a, x * 4 + peers[k]))

    def swap_in(k, n):
        return remote(hb.at[k, pl.ds(3 * n, 3)], blk.at[pl.ds(3 * n, 3), peers[k]], has, har.at[2 * k + n], (a, r))

    def half_of(g, n):
        rows = pl.ds(pl.multiple_of(g * 384, 128), 384)
        cols = slice(n * 128, (n + 1) * 128)
        return dot3(xh[rows, :], xl[rows, :], ch[:, cols], cl[:, cols], NN_DIMS).reshape(3, 128, 128)

    def turn(src, slot, p):
        rows = pl.ds(pl.multiple_of(p * 128, 128), 128)
        for q in range(6):
            high, low = split(src[q, p])
            gg[slot, 0, rows, q * 128:(q + 1) * 128] = high
            gg[slot, 1, rows, q * 128:(q + 1) * 128] = low

    def turn_half(src, start, slot):
        def body(n, _):
            rows = pl.ds(pl.multiple_of(n * 128, 128), 128)
            for q in range(3):
                high, low = split(src[start + q, n])
                eh[slot, 0, rows, q * 128:(q + 1) * 128] = high
                eh[slot, 1, rows, q * 128:(q + 1) * 128] = low
            return 0
        lax.fori_loop(0, 4, body, 0)

    mine = x // 2
    others = x_to // 2

    def whole(p, k, n):
        part = pl.ds(3 * n, 3)
        return remote(blk.at[part, p], xfull.at[part, p], xs.at[0], xr.at[2 * k + n], (a, x_to * 4 + i))

    def part_way(p):
        return remote(blk.at[pl.ds(3 * mine, 3), p], xhalf.at[:, p], xs.at[1], xr.at[8], (a, x_back * 4 + i))

    def get_whole(p, k):
        for n in range(2):
            whole(p, k, n).wait_recv()
        turn(xfull, 1, p)

    def square(n, buf, left, right):
        for jj in range(2):
            cols = slice(jj * 256, (jj + 1) * 256)
            value = dot3(buf[left, 0], buf[left, 1], buf[right, 0, cols, :], buf[right, 1, cols, :], NT_DIMS)
            for m in range(4):
                for jl in range(2):
                    for h in range(2):
                        pc[n, h, m, 2 * jj + jl] = value[
                            m * 128 + h * 64:m * 128 + (h + 1) * 64, jl * 128:(jl + 1) * 128
                        ].reshape(2, 32, 128)

    def core_swap(n):
        return remote(pc.at[n, 1 - c], cb.at[n], ccs, ccr.at[n], (a, r + 1 - 2 * c))

    def core_sum(n):
        core_swap(n).wait_recv()
        for m in range(4):
            pc[n, c, m] = pc[n, c, m] + cb[n, m]

    def fy(d, p):
        py = lax.rem(y + d, 4)
        return remote(pf.at[py, p], ryf.at[d - 1, p], fys, fyr, at(x, py, z, c))

    def fz(d):
        pz = lax.rem(z + d, 8)
        j, f = owned(pz, side)
        return remote(sf.at[2 * j + f], rzf.at[d - 1], fzs, fzr, at(x, y, pz, c))

    def ey(d):
        py = lax.rem(y + d, 4)
        return remote(pc.at[1, c, py], rye.at[d - 1], eys, eyr, at(x, py, z, c))

    def ez(d):
        pz = lax.rem(z + d, 8)
        j, f = owned(pz, side)
        return remote(se_.at[j, f], rze.at[d - 1], ezs, ezr, at(x, y, pz, c))

    def d_own(pz):
        j, f = owned(pz, 1 - side)
        return pc.at[0, c, :, j, f]

    def dz(d):
        pz = lax.rem(z + d, 8)
        return remote(d_own(pz), rzd.at[d - 1], dzs, dzr, at(x, y, pz, c))

    def dy(d):
        py = lax.rem(y + d, 4)
        return remote(sd.at[py], ryd.at[d - 1], dys, dyr, at(x, py, z, c))

    def deliver(n):
        dev, src, dst, sem = outgoing[n]
        return remote(src, dst, fs.at[n], sem, dev)

    def send_out(n):
        dev, src, dst, _ = outgoing[n]

        @pl.when(jnp.logical_not(is_me(dev)))
        def _():
            deliver(n).start()

        if n < 2:
            @pl.when(is_me(dev))
            def _():
                pltpu.make_async_copy(src, dst, outgoing[n][3]).start()

    def f_piece(p, k):
        get_whole(p, k)
        rows = pl.ds(pl.multiple_of(p * 128, 128), 128)
        value = dot3(gg[0, 0], gg[0, 1], gg[1, 0, rows, :], gg[1, 1, rows, :], NT_DIMS)
        for m in range(4):
            pf[m, p] = value[m * 128:(m + 1) * 128].reshape(2, 64, 128)
        for d in (2, 1, 3):
            fy(d, p).start()

    pair = hi * 2

    def f_row(m):
        rows = pl.ds(pl.multiple_of(m * 128, 128), 128)
        cols = pl.ds(pl.multiple_of(pair * 128, 256), 256)
        value = dot3(gg[0, 0, rows, :], gg[0, 1, rows, :], gg[1, 0, cols, :], gg[1, 1, cols, :], NT_DIMS)
        for n in range(2):
            pf[m, pair + n] = value[:, n * 128:(n + 1) * 128].reshape(2, 64, 128)
        d = lax.rem(m + 4 - y, 4)

        @pl.when(d > 0)
        def _():
            for n in range(2):
                fy(d, pair + n).start()

    def half_out(k, n):
        hb[k, 3 * n:3 * n + 3] = half_of(peers[k], n)
        swap(k, n).start()

    def half_own(n):
        blk[3 * n:3 * n + 3, i] = half_of(i, n)
        whole(i, 3, n).start()

    def arrived(k, n):
        swap_in(k, n).wait_recv()
        whole(peers[k], k, n).start()

    take_c(0)
    half_out(0, 0)
    half_own(0)
    half_out(2, 0)
    take_c(1)
    half_out(0, 1)
    half_own(1)
    arrived(2, 0)
    half_out(1, 0)
    half_out(2, 1)
    half_out(1, 1)
    turn(blk, 0, i)
    arrived(2, 1)
    turn(blk, 0, peers[2])
    arrived(0, 0)
    arrived(0, 1)
    turn(blk, 0, peers[0])
    get_whole(i, 3)
    get_whole(peers[2], 2)
    part_way(i).start()
    part_way(peers[2]).start()
    f_row(i)
    f_row(peers[2])
    f_row(peers[0])
    arrived(1, 0)
    part_way(peers[0]).start()
    arrived(1, 1)
    turn(blk, 0, peers[1])
    part_way(peers[1]).start()
    square(0, gg, 0, 0)
    core_swap(0).start()
    f_row(peers[1])
    core_sum(0)
    for d in (4, 3, 5, 2, 6, 1, 7):
        dz(d).start()
    f_piece(peers[0], 0)
    f_piece(peers[1], 1)
    turn_half(xfull, 3 * others, 1 - c)
    took(xr.at[8], xhalf)
    turn_half(xhalf, 0, c)
    square(1, eh, 0, 1)
    core_swap(1).start()
    core_sum(1)
    for d in (2, 1, 3):
        ey(d).start()
    took(fyr, ryf)
    for m in range(4):
        sf[2 * m:2 * m + 2] = pf[y, m] + ryf[0, m] + ryf[1, m] + ryf[2, m]
    for d in (4, 3, 5, 2, 6, 1, 7):
        fz(d).start()
    took(eyr, rye)
    se_[...] = pc[1, c, y] + rye[0] + rye[1] + rye[2]
    for d in (4, 3, 5, 2, 6, 1, 7):
        ez(d).start()
    took(dzr, rzd)
    total = d_own(z)[...]
    for d in range(7):
        total = total + rzd[d]
    sd[...] = total
    for d in (2, 1, 3):
        dy(d).start()
    took(fzr, rzf)
    total = sf[2 * bj + sub]
    for d in range(7):
        total = total + rzf[d]
    redf[...] = total
    send_out(1)
    send_out(2)
    took(dyr, ryd)
    redq[0] = sd[y] + ryd[0] + ryd[1] + ryd[2]
    send_out(0)
    took(ezr, rze)
    total = se_[bj, sub]
    for d in range(7):
        total = total + rze[d]
    redq[1] = total
    send_out(3)
    send_out(4)

    @pl.when(delta == 0)
    def _():
        took(frq.at[0], fin_q.at[0])
        out_ref[...] = fin_q[0].reshape(128, 128)

    @pl.when(turned)
    def _():
        took(frq.at[0], fin_q.at[0])
        took(frq.at[1], fin_q.at[1])
        out_ref[...] = fin_q[0].reshape(128, 128) + fin_q[1].reshape(128, 128).T

    @pl.when(odd)
    def _():
        took(frf.at[0], fin_f.at[0])
        took(frf.at[1], fin_f.at[1])
        out_ref[...] = fin_f[0].reshape(128, 128) + fin_f[1].reshape(128, 128).T

    for sem, ref in (
        (c1s, tslice.at[pl.ds(0, 15)]), (tis, tall.at[pl.ds(0, 15)]), (c2s, picks), (has, hb),
        (xs.at[0], blk), (xs.at[1], xhalf), (ccs, cb), (fys, ryf), (fzs, rzf), (eys, rye), (ezs, rze), (dzs, rzd), (dys, ryd),
    ):
        took(sem, ref)
    for n in range(5):
        @pl.when(jnp.logical_not(is_me(outgoing[n][0])))
        def _():
            deliver(n).wait_send()


def on_device(three_index, coefficients, tile_index):
    dma = pltpu.SemaphoreType.DMA
    vm = pltpu.VMEM
    return pl.pallas_call(
        kernel,
        out_shape=jax.ShapeDtypeStruct((128, 128), F32),
        in_specs=[
            pl.BlockSpec(memory_space=pl.ANY),
            pl.BlockSpec(memory_space=pl.ANY),
            pl.BlockSpec(memory_space=pl.ANY),
        ],
        out_specs=pl.BlockSpec(memory_space=pltpu.VMEM),
        scratch_shapes=[
            vm((1536, 512), F32), vm((1536, 512), BF16), vm((1536, 512), BF16),
            vm((16, 8, 256), F32), vm((8, 128), jnp.int32), vm((16, 8, 128), jnp.int32),
            pltpu.SMEM((16, 128), jnp.int32), pltpu.SMEM((1, 4), jnp.int32),
            vm((15, 2, 4, 8, 128), F32), vm((2, 4, 16, 8, 128), F32),
            vm((512, 256), BF16), vm((512, 256), BF16),
            vm((3, 6, 128, 128), F32), vm((6, 4, 128, 128), F32), vm((6, 4, 128, 128), F32), vm((3, 4, 128, 128), F32),
            vm((2, 2, 512, 768), BF16), vm((2, 2, 512, 384), BF16),
            vm((2, 2, 4, 4, 2, 32, 128), F32), vm((2, 4, 4, 2, 32, 128), F32),
            vm((4, 4, 2, 64, 128), F32), vm((3, 4, 2, 64, 128), F32), vm((8, 64, 128), F32), vm((7, 64, 128), F32),
            vm((64, 128), F32),
            vm((3, 4, 2, 32, 128), F32), vm((4, 2, 32, 128), F32), vm((7, 32, 128), F32),
            vm((7, 4, 32, 128), F32), vm((4, 32, 128), F32), vm((3, 32, 128), F32),
            vm((2, 32, 128), F32), vm((2, 2, 2, 32, 128), F32), vm((2, 2, 64, 128), F32),
            dma((3,)), dma, dma, dma, dma, dma, dma((2,)), dma,
            dma, dma((6,)), dma((2,)), dma((9,)), dma, dma((2,)),
            dma, dma, dma, dma, dma, dma, dma, dma, dma, dma, dma, dma,
            dma((5,)), dma((2,)), dma((2,)),
        ],
        compiler_params=pltpu.CompilerParams(
            collective_id=0, has_side_effects=True, vmem_limit_bytes=55091 * 2**10
        ),
    )(three_index.reshape(1536, 512), coefficients.reshape(16, 8, 256), tile_index)


def solution(mesh):
    return jax.shard_map(
        on_device,
        mesh=mesh,
        in_specs=(P("aux", "row", None), P("aux", None), P("aux", "row", None)),
        out_specs=P("row", "aux"),
        check_vma=False,
    )
```

```python
import functools

import jax
import jax.numpy as jnp
from jax import lax
from jax.experimental import pallas as pl
from jax.experimental.pallas import tpu as pltpu
from jax.sharding import PartitionSpec as P

MESH = pl.DeviceIdType.MESH
F32 = jnp.float32
BF16 = jnp.bfloat16
NT_DIMS = (((1,), (1,)), ((), ()))
NN_DIMS = (((1,), (0,)), ((), ()))


def split(value):
    high = value.astype(BF16)
    return high, (value - high.astype(F32)).astype(BF16)


def dot3(lh, ll, rh, rl, dims):
    dot = functools.partial(lax.dot_general, dimension_numbers=dims, preferred_element_type=F32)
    return dot(lh, rh) + (dot(lh, rl) + dot(ll, rh))


def kernel(
    x_ref, c_ref, t_ref, out_ref,
    xv, xh, xl, tslice, tvec, tall, tsm, tloc, picks, csel, ch, cl,
    hb, blk, xfull, xhalf, gg, eh,
    pc, cb, pf, ryf, sf, rzf, redf, rye, se_, rze, rzd, sd, ryd, redq, fin_q, fin_f,
    loads, c1s, c1r, tis, tir, c2s, c2r, tsem, has, har, xs, xr, ccs, ccr,
    fys, fyr, fzs, fzr, eys, eyr, ezs, ezr, dys, dyr, dzs, dzr, fs, frq, frf,
):
    a = lax.axis_index("aux")
    r = lax.axis_index("row")
    lo, z = a // 8, a % 8
    x, i = r // 4, r % 4
    hi, c = i // 2, i % 2
    y = hi * 2 + lo

    def at(px, py, pz, pc):
        return (py % 2) * 8 + pz, px * 4 + (py // 2) * 2 + pc

    def remote(src, dst, ss, rs, dev):
        return pltpu.make_async_remote_copy(
            src_ref=src, dst_ref=dst, send_sem=ss, recv_sem=rs, device_id=dev, device_id_type=MESH
        )

    def took(sem, ref):
        remote(ref, ref, sem, sem, (a, r)).wait_recv()

    def is_me(dev):
        return (dev[0] == a) & (dev[1] == r)

    barrier = pltpu.get_barrier_semaphore()

    def greet(dev):
        pl.semaphore_signal(barrier, inc=1, device_id=dev, device_id_type=MESH)

    def greet_axes(d, _):
        greet((a, lax.rem(r + d, 16)))
        greet((lax.rem(a + d, 16), r))
        return 0

    lax.fori_loop(1, 16, greet_axes, 0)
    own_c = pltpu.make_async_copy(c_ref.at[r], tslice.at[a], loads.at[1])
    own_t = pltpu.make_async_copy(t_ref.at[0], tloc, loads.at[2])
    own_t.start()
    own_c.start()

    def load_x(n):
        return pltpu.make_async_copy(x_ref.at[pl.ds(n * 384, 384)], xv.at[pl.ds(n * 384, 384)], loads.at[0])

    for n in range(4):
        load_x(n).start()

    def owned(pz, side):
        far = jnp.where(pz // 4 == side, 0, 1)
        return jnp.where(far == 0, pz % 4, 3 - pz % 4), far

    side = (x + 1) % 2
    bi = y
    bj, sub = owned(z, side)
    dj, dsub = owned(z, 1 - side)
    step = 2 * c - 1
    x_to = lax.rem(x + 4 + step, 4)
    x_back = lax.rem(x + 4 - step, 4)
    ea, eb = lax.rem(x + 3, 4), lax.rem(x + 1, 4)
    outgoing = [
        ((x * 4 + dj, x * 4 + bi), redq.at[0], fin_q.at[0, c, dsub], frq.at[0]),
        ((x_back * 4 + bj, x * 4 + bi), redf, fin_f.at[0, sub], frf.at[0]),
        ((x * 4 + bi, x_back * 4 + bj), redf, fin_f.at[1, sub], frf.at[1]),
        ((eb * 4 + bj, ea * 4 + bi), redq.at[1], fin_q.at[0, c, sub], frq.at[0]),
        ((ea * 4 + bi, eb * 4 + bj), redq.at[1], fin_q.at[1, c, sub], frq.at[1]),
    ]
    xc = a // 4
    delta = lax.rem(xc + 4 - x, 4)
    odd = (delta % 2) == 1
    turned = delta == 2

    lane = lax.broadcasted_iota(jnp.int32, (8, 128), 1)
    own_t.wait()
    ids = jnp.zeros((8, 128), jnp.int32)
    for s in range(4):
        ids = jnp.where(lane == s, tloc[0, s], ids)
    tvec[...] = ids
    own_c.wait()
    pl.semaphore_wait(barrier, 30)

    def c1(d):
        return remote(tslice.at[a], tslice.at[a], c1s, c1r, (lax.rem(a + d, 16), r))

    def ti(d):
        return remote(tvec, tall.at[r], tis, tir, (a, lax.rem(r + d, 16)))

    def start1(d, _):
        c1(d).start()
        ti(d).start()
        return 0

    lax.fori_loop(1, 16, start1, 0)
    tall[r] = ids

    def split_x(n, _):
        rows = pl.ds(pl.multiple_of(n * 128, 128), 128)
        high, low = split(xv[rows, :])
        xh[rows, :] = high
        xl[rows, :] = low
        return 0

    pltpu.make_async_copy(x_ref, xv, loads.at[0]).wait()
    lax.fori_loop(0, 12, split_x, 0)

    took(tir, tall.at[pl.ds(0, 15)])
    to_smem = pltpu.make_async_copy(tall.at[:, 0], tsm, tsem)
    to_smem.start()
    to_smem.wait()

    took(c1r, tslice.at[pl.ds(0, 15)])

    def c2(n, d):
        return remote(picks.at[d - 1, n], csel.at[n, :, r], c2s, c2r.at[n], (a, lax.rem(r + d, 16)))

    for n in range(2):
        def start2(d, _):
            who = lax.rem(r + d, 16)
            for s in range(4):
                picks[d - 1, n, s] = tslice[tsm[who, s], :, n * 128:(n + 1) * 128]
            c2(n, d).start()
            return 0

        lax.fori_loop(1, 16, start2, 0)
    for n in range(2):
        for s in range(4):
            csel[n, s, r] = tslice[tsm[r, s], :, n * 128:(n + 1) * 128]

    def take_c(n):
        took(c2r.at[n], picks.at[:, n])
        cols = slice(n * 128, (n + 1) * 128)
        for s in range(4):
            high, low = split(csel[n, s].reshape(128, 128))
            ch[s * 128:(s + 1) * 128, cols] = high
            cl[s * 128:(s + 1) * 128, cols] = low

    peers = [lax.rem(i + 2, 4), 3 - i, i + 1 - 2 * c]

    def swap(k, n):
        return remote(hb.at[k, pl.ds(3 * n, 3)], blk.at[pl.ds(3 * n, 3), i], has, har.at[2 * k + n], (a, x * 4 + peers[k]))

    def swap_in(k, n):
        return remote(hb.at[k, pl.ds(3 * n, 3)], blk.at[pl.ds(3 * n, 3), peers[k]], has, har.at[2 * k + n], (a, r))

    def half_of(g, n):
        rows = pl.ds(pl.multiple_of(g * 384, 128), 384)
        cols = slice(n * 128, (n + 1) * 128)
        return dot3(xh[rows, :], xl[rows, :], ch[:, cols], cl[:, cols], NN_DIMS).reshape(3, 128, 128)

    def turn(src, slot, p, half=None):
        rows = pl.ds(pl.multiple_of(p * 128, 128), 128)
        for q in range(6) if half is None else range(3 * half, 3 * half + 3):
            high, low = split(src[q, p])
            gg[slot, 0, rows, q * 128:(q + 1) * 128] = high
            gg[slot, 1, rows, q * 128:(q + 1) * 128] = low

    def turn_half(src, start, slot):
        def body(n, _):
            rows = pl.ds(pl.multiple_of(n * 128, 128), 128)
            for q in range(3):
                high, low = split(src[start + q, n])
                eh[slot, 0, rows, q * 128:(q + 1) * 128] = high
                eh[slot, 1, rows, q * 128:(q + 1) * 128] = low
            return 0
        lax.fori_loop(0, 4, body, 0)

    mine = x // 2
    others = x_to // 2

    def whole(p, k, n):
        part = pl.ds(3 * n, 3)
        return remote(blk.at[part, p], xfull.at[part, p], xs.at[0], xr.at[2 * k + n], (a, x_to * 4 + i))

    def part_way(p):
        return remote(blk.at[pl.ds(3 * mine, 3), p], xhalf.at[:, p], xs.at[1], xr.at[8], (a, x_back * 4 + i))

    def get_whole(p, k):
        for n in range(2):
            whole(p, k, n).wait_recv()
        turn(xfull, 1, p)

    def square(n, buf, left, right):
        for jj in range(2):
            cols = slice(jj * 256, (jj + 1) * 256)
            value = dot3(buf[left, 0], buf[left, 1], buf[right, 0, cols, :], buf[right, 1, cols, :], NT_DIMS)
            for m in range(4):
                for jl in range(2):
                    for h in range(2):
                        pc[n, h, m, 2 * jj + jl] = value[
                            m * 128 + h * 64:m * 128 + (h + 1) * 64, jl * 128:(jl + 1) * 128
                        ].reshape(2, 32, 128)

    def core_swap(n):
        return remote(pc.at[n, 1 - c], cb.at[n], ccs, ccr.at[n], (a, r + 1 - 2 * c))

    def core_sum(n):
        core_swap(n).wait_recv()
        for m in range(4):
            pc[n, c, m] = pc[n, c, m] + cb[n, m]

    def fy(d, p):
        py = lax.rem(y + d, 4)
        return remote(pf.at[py, p], ryf.at[d - 1, p], fys, fyr, at(x, py, z, c))

    def fz(d):
        pz = lax.rem(z + d, 8)
        j, f = owned(pz, side)
        return remote(sf.at[2 * j + f], rzf.at[d - 1], fzs, fzr, at(x, y, pz, c))

    def ey(d):
        py = lax.rem(y + d, 4)
        return remote(pc.at[1, c, py], rye.at[d - 1], eys, eyr, at(x, py, z, c))

    def ez(d):
        pz = lax.rem(z + d, 8)
        j, f = owned(pz, side)
        return remote(se_.at[j, f], rze.at[d - 1], ezs, ezr, at(x, y, pz, c))

    def d_own(pz):
        j, f = owned(pz, 1 - side)
        return pc.at[0, c, :, j, f]

    def dz(d):
        pz = lax.rem(z + d, 8)
        return remote(d_own(pz), rzd.at[d - 1], dzs, dzr, at(x, y, pz, c))

    def dy(d):
        py = lax.rem(y + d, 4)
        return remote(sd.at[py], ryd.at[d - 1], dys, dyr, at(x, py, z, c))

    def deliver(n):
        dev, src, dst, sem = outgoing[n]
        return remote(src, dst, fs.at[n], sem, dev)

    def send_out(n):
        dev, src, dst, _ = outgoing[n]

        @pl.when(jnp.logical_not(is_me(dev)))
        def _():
            deliver(n).start()

        if n < 2:
            @pl.when(is_me(dev))
            def _():
                pltpu.make_async_copy(src, dst, outgoing[n][3]).start()

    def f_piece(p, k):
        rows = pl.ds(pl.multiple_of(p * 128, 128), 128)
        for n in range(2):
            whole(p, k, n).wait_recv()
            turn(xfull, 1, p, n)
            part = slice(n * 384, (n + 1) * 384)
            value = dot3(gg[0, 0, :, part], gg[0, 1, :, part], gg[1, 0, rows, part], gg[1, 1, rows, part], NT_DIMS)
            for m in range(4):
                block = value[m * 128:(m + 1) * 128].reshape(2, 64, 128)
                pf[m, p] = block if n == 0 else pf[m, p] + block
        for d in (2, 1, 3):
            fy(d, p).start()

    pair = hi * 2

    def f_row(m):
        rows = pl.ds(pl.multiple_of(m * 128, 128), 128)
        cols = pl.ds(pl.multiple_of(pair * 128, 256), 256)
        value = dot3(gg[0, 0, rows, :], gg[0, 1, rows, :], gg[1, 0, cols, :], gg[1, 1, cols, :], NT_DIMS)
        for n in range(2):
            pf[m, pair + n] = value[:, n * 128:(n + 1) * 128].reshape(2, 64, 128)
        d = lax.rem(m + 4 - y, 4)

        @pl.when(d > 0)
        def _():
            for n in range(2):
                fy(d, pair + n).start()

    def half_out(k, n):
        hb[k, 3 * n:3 * n + 3] = half_of(peers[k], n)
        swap(k, n).start()

    def half_own(n):
        blk[3 * n:3 * n + 3, i] = half_of(i, n)
        whole(i, 3, n).start()

        @pl.when(mine == n)
        def _():
            part_way(i).start()


    def arrived(k, n):
        swap_in(k, n).wait_recv()
        whole(peers[k], k, n).start()

    take_c(0)
    half_out(0, 0)
    half_own(0)
    half_out(2, 0)
    take_c(1)
    half_out(0, 1)
    half_own(1)
    arrived(2, 0)
    half_out(1, 0)
    half_out(2, 1)
    half_out(1, 1)
    turn(blk, 0, i)
    arrived(2, 1)
    turn(blk, 0, peers[2])
    arrived(0, 0)
    arrived(0, 1)
    turn(blk, 0, peers[0])
    get_whole(i, 3)
    get_whole(peers[2], 2)
    part_way(peers[2]).start()
    f_row(i)
    f_row(peers[2])
    f_row(peers[0])
    arrived(1, 0)
    part_way(peers[0]).start()
    arrived(1, 1)
    turn(blk, 0, peers[1])
    part_way(peers[1]).start()
    square(0, gg, 0, 0)
    core_swap(0).start()
    f_row(peers[1])
    core_sum(0)
    for d in (4, 3, 5, 2, 6, 1, 7):
        dz(d).start()
    f_piece(peers[0], 0)
    f_piece(peers[1], 1)
    turn_half(xfull, 3 * others, 1 - c)
    took(xr.at[8], xhalf)
    turn_half(xhalf, 0, c)
    square(1, eh, 0, 1)
    core_swap(1).start()
    core_sum(1)
    for d in (2, 1, 3):
        ey(d).start()
    took(fyr, ryf)
    for m in range(4):
        sf[2 * m:2 * m + 2] = pf[y, m] + ryf[0, m] + ryf[1, m] + ryf[2, m]
    for d in (4, 3, 5, 2, 6, 1, 7):
        fz(d).start()
    took(eyr, rye)
    se_[...] = pc[1, c, y] + rye[0] + rye[1] + rye[2]
    for d in (4, 3, 5, 2, 6, 1, 7):
        ez(d).start()
    took(dzr, rzd)
    total = d_own(z)[...]
    for d in range(7):
        total = total + rzd[d]
    sd[...] = total
    for d in (2, 1, 3):
        dy(d).start()
    took(fzr, rzf)
    total = sf[2 * bj + sub]
    for d in range(7):
        total = total + rzf[d]
    redf[...] = total
    send_out(1)
    send_out(2)
    took(dyr, ryd)
    redq[0] = sd[y] + ryd[0] + ryd[1] + ryd[2]
    send_out(0)
    took(ezr, rze)
    total = se_[bj, sub]
    for d in range(7):
        total = total + rze[d]
    redq[1] = total
    send_out(3)
    send_out(4)

    @pl.when(delta == 0)
    def _():
        took(frq.at[0], fin_q.at[0])
        out_ref[...] = fin_q[0].reshape(128, 128)

    @pl.when(turned)
    def _():
        took(frq.at[0], fin_q.at[0])
        took(frq.at[1], fin_q.at[1])
        out_ref[...] = fin_q[0].reshape(128, 128) + fin_q[1].reshape(128, 128).T

    @pl.when(odd)
    def _():
        took(frf.at[0], fin_f.at[0])
        took(frf.at[1], fin_f.at[1])
        out_ref[...] = fin_f[0].reshape(128, 128) + fin_f[1].reshape(128, 128).T

    for sem, ref in (
        (c1s, tslice.at[pl.ds(0, 15)]), (tis, tall.at[pl.ds(0, 15)]), (c2s, picks), (has, hb),
        (xs.at[0], blk), (xs.at[1], xhalf), (ccs, cb), (fys, ryf), (fzs, rzf), (eys, rye), (ezs, rze), (dzs, rzd), (dys, ryd),
    ):
        took(sem, ref)
    for n in range(5):
        @pl.when(jnp.logical_not(is_me(outgoing[n][0])))
        def _():
            deliver(n).wait_send()


def on_device(three_index, coefficients, tile_index):
    dma = pltpu.SemaphoreType.DMA
    vm = pltpu.VMEM
    return pl.pallas_call(
        kernel,
        out_shape=jax.ShapeDtypeStruct((128, 128), F32),
        in_specs=[
            pl.BlockSpec(memory_space=pl.ANY),
            pl.BlockSpec(memory_space=pl.ANY),
            pl.BlockSpec(memory_space=pl.ANY),
        ],
        out_specs=pl.BlockSpec(memory_space=pltpu.VMEM),
        scratch_shapes=[
            vm((1536, 512), F32), vm((1536, 512), BF16), vm((1536, 512), BF16),
            vm((16, 8, 256), F32), vm((8, 128), jnp.int32), vm((16, 8, 128), jnp.int32),
            pltpu.SMEM((16, 128), jnp.int32), pltpu.SMEM((1, 4), jnp.int32),
            vm((15, 2, 4, 8, 128), F32), vm((2, 4, 16, 8, 128), F32),
            vm((512, 256), BF16), vm((512, 256), BF16),
            vm((3, 6, 128, 128), F32), vm((6, 4, 128, 128), F32), vm((6, 4, 128, 128), F32), vm((3, 4, 128, 128), F32),
            vm((2, 2, 512, 768), BF16), vm((2, 2, 512, 384), BF16),
            vm((2, 2, 4, 4, 2, 32, 128), F32), vm((2, 4, 4, 2, 32, 128), F32),
            vm((4, 4, 2, 64, 128), F32), vm((3, 4, 2, 64, 128), F32), vm((8, 64, 128), F32), vm((7, 64, 128), F32),
            vm((64, 128), F32),
            vm((3, 4, 2, 32, 128), F32), vm((4, 2, 32, 128), F32), vm((7, 32, 128), F32),
            vm((7, 4, 32, 128), F32), vm((4, 32, 128), F32), vm((3, 32, 128), F32),
            vm((2, 32, 128), F32), vm((2, 2, 2, 32, 128), F32), vm((2, 2, 64, 128), F32),
            dma((3,)), dma, dma, dma, dma, dma, dma((2,)), dma,
            dma, dma((6,)), dma((2,)), dma((9,)), dma, dma((2,)),
            dma, dma, dma, dma, dma, dma, dma, dma, dma, dma, dma, dma,
            dma((5,)), dma((2,)), dma((2,)),
        ],
        compiler_params=pltpu.CompilerParams(
            collective_id=0, has_side_effects=True, vmem_limit_bytes=55091 * 2**10
        ),
    )(three_index.reshape(1536, 512), coefficients.reshape(16, 8, 256), tile_index)


def solution(mesh):
    return jax.shard_map(
        on_device,
        mesh=mesh,
        in_specs=(P("aux", "row", None), P("aux", None), P("aux", "row", None)),
        out_specs=P("row", "aux"),
        check_vma=False,
    )
```

```python
import functools

import jax
import jax.numpy as jnp
from jax import lax
from jax.experimental import pallas as pl
from jax.experimental.pallas import tpu as pltpu
from jax.sharding import PartitionSpec as P

MESH = pl.DeviceIdType.MESH
F32 = jnp.float32
BF16 = jnp.bfloat16
AUX_ORDER = (12, 4, 11, 13, 5, 3, 10, 14, 6, 2, 9, 15, 7, 1, 8)
ROW_ORDER = (10, 6, 11, 9, 7, 8, 5, 2, 14, 13, 3, 12, 4, 15, 1)
NT_DIMS = (((1,), (1,)), ((), ()))
NN_DIMS = (((1,), (0,)), ((), ()))


def split(value):
    high = value.astype(BF16)
    return high, (value - high.astype(F32)).astype(BF16)


def dot3(lh, ll, rh, rl, dims):
    dot = functools.partial(lax.dot_general, dimension_numbers=dims, preferred_element_type=F32)
    return dot(lh, rh) + (dot(lh, rl) + dot(ll, rh))


def kernel(
    x_ref, c_ref, t_ref, out_ref,
    xv, xh, xl, tslice, tvec, tall, tsm, tloc, picks, csel, ch, cl,
    hb, blk, xfull, xhalf, gg, eh,
    pc, cb, pf, ryf, sf, rzf, redf, rye, se_, rze, rzd, sd, ryd, redq, fin_q, fin_f,
    loads, c1s, c1r, tis, tir, c2s, c2r, tsem, has, har, xs, xr, ccs, ccr,
    fys, fyr, fzs, fzr, eys, eyr, ezs, ezr, dys, dyr, dzs, dzr, fs, frq, frf,
):
    a = lax.axis_index("aux")
    r = lax.axis_index("row")
    lo, z = a // 8, a % 8
    x, i = r // 4, r % 4
    hi, c = i // 2, i % 2
    y = hi * 2 + lo

    def at(px, py, pz, pc):
        return (py % 2) * 8 + pz, px * 4 + (py // 2) * 2 + pc

    def remote(src, dst, ss, rs, dev):
        return pltpu.make_async_remote_copy(
            src_ref=src, dst_ref=dst, send_sem=ss, recv_sem=rs, device_id=dev, device_id_type=MESH
        )

    def took(sem, ref):
        remote(ref, ref, sem, sem, (a, r)).wait_recv()

    def is_me(dev):
        return (dev[0] == a) & (dev[1] == r)

    barrier = pltpu.get_barrier_semaphore()

    def greet(dev):
        pl.semaphore_signal(barrier, inc=1, device_id=dev, device_id_type=MESH)

    for d in AUX_ORDER:
        greet((lax.rem(a + d, 16), r))
    for d in ROW_ORDER:
        greet((a, lax.rem(r + d, 16)))
    own_c = pltpu.make_async_copy(c_ref.at[r], tslice.at[a], loads.at[1])
    own_t = pltpu.make_async_copy(t_ref.at[0], tloc, loads.at[2])
    own_t.start()
    own_c.start()

    def load_x(n):
        return pltpu.make_async_copy(x_ref.at[pl.ds(n * 384, 384)], xv.at[pl.ds(n * 384, 384)], loads.at[0])

    for n in range(4):
        load_x(n).start()

    def owned(pz, side):
        far = jnp.where(pz // 4 == side, 0, 1)
        return jnp.where(far == 0, pz % 4, 3 - pz % 4), far

    side = (x + 1) % 2
    bi = y
    bj, sub = owned(z, side)
    dj, dsub = owned(z, 1 - side)
    step = 2 * c - 1
    x_to = lax.rem(x + 4 + step, 4)
    x_back = lax.rem(x + 4 - step, 4)
    ea, eb = lax.rem(x + 3, 4), lax.rem(x + 1, 4)
    outgoing = [
        ((x * 4 + dj, x * 4 + bi), redq.at[0], fin_q.at[0, c, dsub], frq.at[0]),
        ((x_back * 4 + bj, x * 4 + bi), redf, fin_f.at[0, sub], frf.at[0]),
        ((x * 4 + bi, x_back * 4 + bj), redf, fin_f.at[1, sub], frf.at[1]),
        ((eb * 4 + bj, ea * 4 + bi), redq.at[1], fin_q.at[0, c, sub], frq.at[0]),
        ((ea * 4 + bi, eb * 4 + bj), redq.at[1], fin_q.at[1, c, sub], frq.at[1]),
    ]
    xc = a // 4
    delta = lax.rem(xc + 4 - x, 4)
    odd = (delta % 2) == 1
    turned = delta == 2

    lane = lax.broadcasted_iota(jnp.int32, (8, 128), 1)
    own_t.wait()
    ids = jnp.zeros((8, 128), jnp.int32)
    for s in range(4):
        ids = jnp.where(lane == s, tloc[0, s], ids)
    tvec[...] = ids
    own_c.wait()
    pl.semaphore_wait(barrier, 30)

    def c1(d):
        return remote(tslice.at[a], tslice.at[a], c1s, c1r, (lax.rem(a + d, 16), r))

    def ti(d):
        return remote(tvec, tall.at[r], tis, tir, (a, lax.rem(r + d, 16)))

    for d in AUX_ORDER:
        c1(d).start()
    for d in ROW_ORDER:
        ti(d).start()
    tall[r] = ids

    def split_x(n, _):
        rows = pl.ds(pl.multiple_of(n * 128, 128), 128)
        high, low = split(xv[rows, :])
        xh[rows, :] = high
        xl[rows, :] = low
        return 0

    pltpu.make_async_copy(x_ref, xv, loads.at[0]).wait()
    lax.fori_loop(0, 12, split_x, 0)

    took(tir, tall.at[pl.ds(0, 15)])
    to_smem = pltpu.make_async_copy(tall.at[:, 0], tsm, tsem)
    to_smem.start()
    to_smem.wait()

    took(c1r, tslice.at[pl.ds(0, 15)])

    def c2(n, d):
        return remote(picks.at[d - 1, n], csel.at[n, :, r], c2s, c2r.at[n], (a, lax.rem(r + d, 16)))

    for n in range(2):
        def start2(d, _):
            who = lax.rem(r + d, 16)
            for s in range(4):
                picks[d - 1, n, s] = tslice[tsm[who, s], :, n * 128:(n + 1) * 128]
            c2(n, d).start()
            return 0

        lax.fori_loop(1, 16, start2, 0)
    for n in range(2):
        for s in range(4):
            csel[n, s, r] = tslice[tsm[r, s], :, n * 128:(n + 1) * 128]

    def take_c(n):
        took(c2r.at[n], picks.at[:, n])
        cols = slice(n * 128, (n + 1) * 128)
        for s in range(4):
            high, low = split(csel[n, s].reshape(128, 128))
            ch[s * 128:(s + 1) * 128, cols] = high
            cl[s * 128:(s + 1) * 128, cols] = low

    peers = [lax.rem(i + 2, 4), 3 - i, i + 1 - 2 * c]

    def swap(k, n):
        return remote(hb.at[k, pl.ds(3 * n, 3)], blk.at[pl.ds(3 * n, 3), i], has, har.at[2 * k + n], (a, x * 4 + peers[k]))

    def swap_in(k, n):
        return remote(hb.at[k, pl.ds(3 * n, 3)], blk.at[pl.ds(3 * n, 3), peers[k]], has, har.at[2 * k + n], (a, r))

    def half_of(g, n):
        rows = pl.ds(pl.multiple_of(g * 384, 128), 384)
        cols = slice(n * 128, (n + 1) * 128)
        return dot3(xh[rows, :], xl[rows, :], ch[:, cols], cl[:, cols], NN_DIMS).reshape(3, 128, 128)

    def turn(src, slot, p, half=None):
        rows = pl.ds(pl.multiple_of(p * 128, 128), 128)
        for q in range(6) if half is None else range(3 * half, 3 * half + 3):
            high, low = split(src[q, p])
            gg[slot, 0, rows, q * 128:(q + 1) * 128] = high
            gg[slot, 1, rows, q * 128:(q + 1) * 128] = low

    def turn_half(src, start, slot):
        def body(n, _):
            rows = pl.ds(pl.multiple_of(n * 128, 128), 128)
            for q in range(3):
                high, low = split(src[start + q, n])
                eh[slot, 0, rows, q * 128:(q + 1) * 128] = high
                eh[slot, 1, rows, q * 128:(q + 1) * 128] = low
            return 0
        lax.fori_loop(0, 4, body, 0)

    mine = x // 2
    others = x_to // 2

    def whole(p, k, n):
        part = pl.ds(3 * n, 3)
        return remote(blk.at[part, p], xfull.at[part, p], xs.at[0], xr.at[2 * k + n], (a, x_to * 4 + i))

    def part_way(p):
        return remote(blk.at[pl.ds(3 * mine, 3), p], xhalf.at[:, p], xs.at[1], xr.at[8], (a, x_back * 4 + i))

    def get_whole(p, k):
        for n in range(2):
            whole(p, k, n).wait_recv()
        turn(xfull, 1, p)

    def square(n, buf, left, right):
        for jj in range(2):
            cols = slice(jj * 256, (jj + 1) * 256)
            value = dot3(buf[left, 0], buf[left, 1], buf[right, 0, cols, :], buf[right, 1, cols, :], NT_DIMS)
            for m in range(4):
                for jl in range(2):
                    for h in range(2):
                        pc[n, h, m, 2 * jj + jl] = value[
                            m * 128 + h * 64:m * 128 + (h + 1) * 64, jl * 128:(jl + 1) * 128
                        ].reshape(2, 32, 128)

    def core_swap(n):
        return remote(pc.at[n, 1 - c], cb.at[n], ccs, ccr.at[n], (a, r + 1 - 2 * c))

    def core_sum(n):
        core_swap(n).wait_recv()
        for m in range(4):
            pc[n, c, m] = pc[n, c, m] + cb[n, m]

    def fy(d, p):
        py = lax.rem(y + d, 4)
        return remote(pf.at[py, p], ryf.at[d - 1, p], fys, fyr, at(x, py, z, c))

    def fz(d):
        pz = lax.rem(z + d, 8)
        j, f = owned(pz, side)
        return remote(sf.at[2 * j + f], rzf.at[d - 1], fzs, fzr, at(x, y, pz, c))

    def ey(d):
        py = lax.rem(y + d, 4)
        return remote(pc.at[1, c, py], rye.at[d - 1], eys, eyr, at(x, py, z, c))

    def ez(d):
        pz = lax.rem(z + d, 8)
        j, f = owned(pz, side)
        return remote(se_.at[j, f], rze.at[d - 1], ezs, ezr, at(x, y, pz, c))

    def d_own(pz):
        j, f = owned(pz, 1 - side)
        return pc.at[0, c, :, j, f]

    def dz(d):
        pz = lax.rem(z + d, 8)
        return remote(d_own(pz), rzd.at[d - 1], dzs, dzr, at(x, y, pz, c))

    def dy(d):
        py = lax.rem(y + d, 4)
        return remote(sd.at[py], ryd.at[d - 1], dys, dyr, at(x, py, z, c))

    def deliver(n):
        dev, src, dst, sem = outgoing[n]
        return remote(src, dst, fs.at[n], sem, dev)

    def send_out(n):
        dev, src, dst, _ = outgoing[n]

        @pl.when(jnp.logical_not(is_me(dev)))
        def _():
            deliver(n).start()

        if n < 2:
            @pl.when(is_me(dev))
            def _():
                pltpu.make_async_copy(src, dst, outgoing[n][3]).start()

    def f_piece(p, k):
        rows = pl.ds(pl.multiple_of(p * 128, 128), 128)
        for n in range(2):
            whole(p, k, n).wait_recv()
            turn(xfull, 1, p, n)
            part = slice(n * 384, (n + 1) * 384)
            value = dot3(gg[0, 0, :, part], gg[0, 1, :, part], gg[1, 0, rows, part], gg[1, 1, rows, part], NT_DIMS)
            for m in range(4):
                block = value[m * 128:(m + 1) * 128].reshape(2, 64, 128)
                pf[m, p] = block if n == 0 else pf[m, p] + block
        for d in (2, 1, 3):
            fy(d, p).start()

    pair = hi * 2

    def f_row(m):
        rows = pl.ds(pl.multiple_of(m * 128, 128), 128)
        cols = pl.ds(pl.multiple_of(pair * 128, 256), 256)
        value = dot3(gg[0, 0, rows, :], gg[0, 1, rows, :], gg[1, 0, cols, :], gg[1, 1, cols, :], NT_DIMS)
        for n in range(2):
            pf[m, pair + n] = value[:, n * 128:(n + 1) * 128].reshape(2, 64, 128)
        d = lax.rem(m + 4 - y, 4)

        @pl.when(d > 0)
        def _():
            for n in range(2):
                fy(d, pair + n).start()

    def half_out(k, n):
        hb[k, 3 * n:3 * n + 3] = half_of(peers[k], n)
        swap(k, n).start()

    def half_own(n):
        blk[3 * n:3 * n + 3, i] = half_of(i, n)
        whole(i, 3, n).start()

        @pl.when(mine == n)
        def _():
            part_way(i).start()


    def arrived(k, n):
        swap_in(k, n).wait_recv()
        whole(peers[k], k, n).start()

    take_c(0)
    half_out(0, 0)
    half_own(0)
    half_out(2, 0)
    take_c(1)
    half_out(0, 1)
    half_own(1)
    arrived(2, 0)
    half_out(1, 0)
    half_out(2, 1)
    half_out(1, 1)
    turn(blk, 0, i)
    arrived(2, 1)
    turn(blk, 0, peers[2])
    arrived(0, 0)
    arrived(0, 1)
    turn(blk, 0, peers[0])
    get_whole(i, 3)
    get_whole(peers[2], 2)
    part_way(peers[2]).start()
    f_row(i)
    f_row(peers[2])
    f_row(peers[0])
    arrived(1, 0)
    part_way(peers[0]).start()
    arrived(1, 1)
    turn(blk, 0, peers[1])
    part_way(peers[1]).start()
    square(0, gg, 0, 0)
    core_swap(0).start()
    f_row(peers[1])
    core_sum(0)
    for d in (4, 3, 5, 2, 6, 1, 7):
        dz(d).start()
    f_piece(peers[0], 0)
    f_piece(peers[1], 1)
    turn_half(xfull, 3 * others, 1 - c)
    took(xr.at[8], xhalf)
    turn_half(xhalf, 0, c)
    square(1, eh, 0, 1)
    core_swap(1).start()
    core_sum(1)
    for d in (2, 1, 3):
        ey(d).start()
    took(fyr, ryf)
    for m in range(4):
        sf[2 * m:2 * m + 2] = pf[y, m] + ryf[0, m] + ryf[1, m] + ryf[2, m]
    for d in (4, 3, 5, 2, 6, 1, 7):
        fz(d).start()
    took(eyr, rye)
    se_[...] = pc[1, c, y] + rye[0] + rye[1] + rye[2]
    for d in (4, 3, 5, 2, 6, 1, 7):
        ez(d).start()
    took(dzr, rzd)
    total = d_own(z)[...]
    for d in range(7):
        total = total + rzd[d]
    sd[...] = total
    for d in (2, 1, 3):
        dy(d).start()
    took(fzr, rzf)
    total = sf[2 * bj + sub]
    for d in range(7):
        total = total + rzf[d]
    redf[...] = total
    send_out(1)
    send_out(2)
    took(dyr, ryd)
    redq[0] = sd[y] + ryd[0] + ryd[1] + ryd[2]
    send_out(0)
    took(ezr, rze)
    total = se_[bj, sub]
    for d in range(7):
        total = total + rze[d]
    redq[1] = total
    send_out(3)
    send_out(4)

    @pl.when(delta == 0)
    def _():
        took(frq.at[0], fin_q.at[0])
        out_ref[...] = fin_q[0].reshape(128, 128)

    @pl.when(turned)
    def _():
        took(frq.at[0], fin_q.at[0])
        took(frq.at[1], fin_q.at[1])
        out_ref[...] = fin_q[0].reshape(128, 128) + fin_q[1].reshape(128, 128).T

    @pl.when(odd)
    def _():
        took(frf.at[0], fin_f.at[0])
        took(frf.at[1], fin_f.at[1])
        out_ref[...] = fin_f[0].reshape(128, 128) + fin_f[1].reshape(128, 128).T

    for sem, ref in (
        (c1s, tslice.at[pl.ds(0, 15)]), (tis, tall.at[pl.ds(0, 15)]), (c2s, picks), (has, hb),
        (xs.at[0], blk), (xs.at[1], xhalf), (ccs, cb), (fys, ryf), (fzs, rzf), (eys, rye), (ezs, rze), (dzs, rzd), (dys, ryd),
    ):
        took(sem, ref)
    for n in range(5):
        @pl.when(jnp.logical_not(is_me(outgoing[n][0])))
        def _():
            deliver(n).wait_send()


def on_device(three_index, coefficients, tile_index):
    dma = pltpu.SemaphoreType.DMA
    vm = pltpu.VMEM
    return pl.pallas_call(
        kernel,
        out_shape=jax.ShapeDtypeStruct((128, 128), F32),
        in_specs=[
            pl.BlockSpec(memory_space=pl.ANY),
            pl.BlockSpec(memory_space=pl.ANY),
            pl.BlockSpec(memory_space=pl.ANY),
        ],
        out_specs=pl.BlockSpec(memory_space=pltpu.VMEM),
        scratch_shapes=[
            vm((1536, 512), F32), vm((1536, 512), BF16), vm((1536, 512), BF16),
            vm((16, 8, 256), F32), vm((8, 128), jnp.int32), vm((16, 8, 128), jnp.int32),
            pltpu.SMEM((16, 128), jnp.int32), pltpu.SMEM((1, 4), jnp.int32),
            vm((15, 2, 4, 8, 128), F32), vm((2, 4, 16, 8, 128), F32),
            vm((512, 256), BF16), vm((512, 256), BF16),
            vm((3, 6, 128, 128), F32), vm((6, 4, 128, 128), F32), vm((6, 4, 128, 128), F32), vm((3, 4, 128, 128), F32),
            vm((2, 2, 512, 768), BF16), vm((2, 2, 512, 384), BF16),
            vm((2, 2, 4, 4, 2, 32, 128), F32), vm((2, 4, 4, 2, 32, 128), F32),
            vm((4, 4, 2, 64, 128), F32), vm((3, 4, 2, 64, 128), F32), vm((8, 64, 128), F32), vm((7, 64, 128), F32),
            vm((64, 128), F32),
            vm((3, 4, 2, 32, 128), F32), vm((4, 2, 32, 128), F32), vm((7, 32, 128), F32),
            vm((7, 4, 32, 128), F32), vm((4, 32, 128), F32), vm((3, 32, 128), F32),
            vm((2, 32, 128), F32), vm((2, 2, 2, 32, 128), F32), vm((2, 2, 64, 128), F32),
            dma((3,)), dma, dma, dma, dma, dma, dma((2,)), dma,
            dma, dma((6,)), dma((2,)), dma((9,)), dma, dma((2,)),
            dma, dma, dma, dma, dma, dma, dma, dma, dma, dma, dma, dma,
            dma((5,)), dma((2,)), dma((2,)),
        ],
        compiler_params=pltpu.CompilerParams(
            collective_id=0, has_side_effects=True, vmem_limit_bytes=55091 * 2**10
        ),
    )(three_index.reshape(1536, 512), coefficients.reshape(16, 8, 256), tile_index)


def solution(mesh):
    return jax.shard_map(
        on_device,
        mesh=mesh,
        in_specs=(P("aux", "row", None), P("aux", None), P("aux", "row", None)),
        out_specs=P("row", "aux"),
        check_vma=False,
    )
```

```python
import functools

import jax
import jax.numpy as jnp
from jax import lax
from jax.experimental import pallas as pl
from jax.experimental.pallas import tpu as pltpu
from jax.sharding import PartitionSpec as P

MESH = pl.DeviceIdType.MESH
F32 = jnp.float32
BF16 = jnp.bfloat16
AUX_ORDER = (12, 4, 11, 13, 5, 3, 10, 14, 6, 2, 9, 15, 7, 1, 8)
ROW_ORDER = (10, 6, 11, 9, 7, 8, 5, 2, 14, 13, 3, 12, 4, 15, 1)
NT_DIMS = (((1,), (1,)), ((), ()))
NN_DIMS = (((1,), (0,)), ((), ()))


def split(value):
    high = value.astype(BF16)
    return high, (value - high.astype(F32)).astype(BF16)


def dot3(lh, ll, rh, rl, dims):
    dot = functools.partial(lax.dot_general, dimension_numbers=dims, preferred_element_type=F32)
    return dot(lh, rh) + (dot(lh, rl) + dot(ll, rh))


def kernel(
    x_ref, c_ref, t_ref, out_ref,
    xv, xh, xl, tslice, tvec, tall, tsm, tloc, picks, csel, ch, cl,
    hb, blk, xfull, xhalf, gg, eh,
    pc, cb, pf, ryf, sf, rzf, redf, rye, se_, rze, rzd, sd, ryd, redq, fin_q, fin_f,
    loads, c1s, c1r, tis, tir, c2s, c2r, tsem, has, har, xs, xr, ccs, ccr,
    fys, fyr, fzs, fzr, eys, eyr, ezs, ezr, dys, dyr, dzs, dzr, fs, frq, frf,
):
    a = lax.axis_index("aux")
    r = lax.axis_index("row")
    lo, z = a // 8, a % 8
    x, i = r // 4, r % 4
    hi, c = i // 2, i % 2
    y = hi * 2 + lo

    def at(px, py, pz, pc):
        return (py % 2) * 8 + pz, px * 4 + (py // 2) * 2 + pc

    def remote(src, dst, ss, rs, dev):
        return pltpu.make_async_remote_copy(
            src_ref=src, dst_ref=dst, send_sem=ss, recv_sem=rs, device_id=dev, device_id_type=MESH
        )

    def took(sem, ref):
        remote(ref, ref, sem, sem, (a, r)).wait_recv()

    def is_me(dev):
        return (dev[0] == a) & (dev[1] == r)

    barrier = pltpu.get_barrier_semaphore()

    def greet(dev):
        pl.semaphore_signal(barrier, inc=1, device_id=dev, device_id_type=MESH)

    for d in AUX_ORDER:
        greet((lax.rem(a + d, 16), r))
    for d in ROW_ORDER:
        greet((a, lax.rem(r + d, 16)))
    own_c = pltpu.make_async_copy(c_ref.at[r], tslice.at[a], loads.at[1])
    own_t = pltpu.make_async_copy(t_ref.at[0], tloc, loads.at[2])
    own_t.start()
    own_c.start()

    def load_x(n):
        return pltpu.make_async_copy(x_ref.at[pl.ds(n * 384, 384)], xv.at[pl.ds(n * 384, 384)], loads.at[0])

    for n in range(4):
        load_x(n).start()

    def owned(pz, side):
        far = jnp.where(pz // 4 == side, 0, 1)
        return jnp.where(far == 0, pz % 4, 3 - pz % 4), far

    side = (x + 1) % 2
    bi = y
    bj, sub = owned(z, side)
    dj, dsub = owned(z, 1 - side)
    step = 2 * c - 1
    x_to = lax.rem(x + 4 + step, 4)
    x_back = lax.rem(x + 4 - step, 4)
    ea, eb = lax.rem(x + 3, 4), lax.rem(x + 1, 4)
    outgoing = [
        ((x * 4 + dj, x * 4 + bi), redq.at[0], fin_q.at[0, c, dsub], frq.at[0]),
        ((x_back * 4 + bj, x * 4 + bi), redf, fin_f.at[0, sub], frf.at[0]),
        ((x * 4 + bi, x_back * 4 + bj), redf, fin_f.at[1, sub], frf.at[1]),
        ((eb * 4 + bj, ea * 4 + bi), redq.at[1], fin_q.at[0, c, sub], frq.at[0]),
        ((ea * 4 + bi, eb * 4 + bj), redq.at[1], fin_q.at[1, c, sub], frq.at[1]),
    ]
    xc = a // 4
    delta = lax.rem(xc + 4 - x, 4)
    odd = (delta % 2) == 1
    turned = delta == 2

    lane = lax.broadcasted_iota(jnp.int32, (8, 128), 1)
    own_t.wait()
    ids = jnp.zeros((8, 128), jnp.int32)
    for s in range(4):
        ids = jnp.where(lane == s, tloc[0, s], ids)
    tvec[...] = ids
    own_c.wait()
    pl.semaphore_wait(barrier, 30)

    def c1(d):
        return remote(tslice.at[a], tslice.at[a], c1s, c1r, (lax.rem(a + d, 16), r))

    def ti(d):
        return remote(tvec, tall.at[r], tis, tir, (a, lax.rem(r + d, 16)))

    for d in AUX_ORDER:
        c1(d).start()
    for d in ROW_ORDER:
        ti(d).start()
    tall[r] = ids

    def split_x(n, _):
        rows = pl.ds(pl.multiple_of(n * 128, 128), 128)
        high, low = split(xv[rows, :])
        xh[rows, :] = high
        xl[rows, :] = low
        return 0

    pltpu.make_async_copy(x_ref, xv, loads.at[0]).wait()
    lax.fori_loop(0, 12, split_x, 0)

    took(tir, tall.at[pl.ds(0, 15)])
    to_smem = pltpu.make_async_copy(tall.at[:, 0], tsm, tsem)
    to_smem.start()
    to_smem.wait()

    took(c1r, tslice.at[pl.ds(0, 15)])

    def c2(n, d):
        return remote(picks.at[d - 1, n], csel.at[n, :, r], c2s, c2r.at[n], (a, lax.rem(r + d, 16)))

    for n in range(2):
        for d in ROW_ORDER:
            who = lax.rem(r + d, 16)
            for s in range(4):
                picks[d - 1, n, s] = tslice[tsm[who, s], :, n * 128:(n + 1) * 128]
            c2(n, d).start()
    for n in range(2):
        for s in range(4):
            csel[n, s, r] = tslice[tsm[r, s], :, n * 128:(n + 1) * 128]

    def take_c(n):
        took(c2r.at[n], picks.at[:, n])
        cols = slice(n * 128, (n + 1) * 128)
        for s in range(4):
            high, low = split(csel[n, s].reshape(128, 128))
            ch[s * 128:(s + 1) * 128, cols] = high
            cl[s * 128:(s + 1) * 128, cols] = low

    peers = [lax.rem(i + 2, 4), 3 - i, i + 1 - 2 * c]

    def swap(k, n):
        return remote(hb.at[k, pl.ds(3 * n, 3)], blk.at[pl.ds(3 * n, 3), i], has, har.at[2 * k + n], (a, x * 4 + peers[k]))

    def swap_in(k, n):
        return remote(hb.at[k, pl.ds(3 * n, 3)], blk.at[pl.ds(3 * n, 3), peers[k]], has, har.at[2 * k + n], (a, r))

    def half_of(g, n):
        rows = pl.ds(pl.multiple_of(g * 384, 128), 384)
        cols = slice(n * 128, (n + 1) * 128)
        return dot3(xh[rows, :], xl[rows, :], ch[:, cols], cl[:, cols], NN_DIMS).reshape(3, 128, 128)

    def turn(src, slot, p, half=None):
        rows = pl.ds(pl.multiple_of(p * 128, 128), 128)
        for q in range(6) if half is None else range(3 * half, 3 * half + 3):
            high, low = split(src[q, p])
            gg[slot, 0, rows, q * 128:(q + 1) * 128] = high
            gg[slot, 1, rows, q * 128:(q + 1) * 128] = low

    def turn_half(src, start, slot):
        def body(n, _):
            rows = pl.ds(pl.multiple_of(n * 128, 128), 128)
            for q in range(3):
                high, low = split(src[start + q, n])
                eh[slot, 0, rows, q * 128:(q + 1) * 128] = high
                eh[slot, 1, rows, q * 128:(q + 1) * 128] = low
            return 0
        lax.fori_loop(0, 4, body, 0)

    mine = x // 2
    others = x_to // 2

    def whole(p, k, n):
        part = pl.ds(3 * n, 3)
        return remote(blk.at[part, p], xfull.at[part, p], xs.at[0], xr.at[2 * k + n], (a, x_to * 4 + i))

    def part_way(p):
        return remote(blk.at[pl.ds(3 * mine, 3), p], xhalf.at[:, p], xs.at[1], xr.at[8], (a, x_back * 4 + i))

    def get_whole(p, k):
        for n in range(2):
            whole(p, k, n).wait_recv()
        turn(xfull, 1, p)

    def square(n, buf, left, right):
        for jj in range(2):
            cols = slice(jj * 256, (jj + 1) * 256)
            value = dot3(buf[left, 0], buf[left, 1], buf[right, 0, cols, :], buf[right, 1, cols, :], NT_DIMS)
            for m in range(4):
                for jl in range(2):
                    for h in range(2):
                        pc[n, h, m, 2 * jj + jl] = value[
                            m * 128 + h * 64:m * 128 + (h + 1) * 64, jl * 128:(jl + 1) * 128
                        ].reshape(2, 32, 128)

    def core_swap(n):
        return remote(pc.at[n, 1 - c], cb.at[n], ccs, ccr.at[n], (a, r + 1 - 2 * c))

    def core_sum(n):
        core_swap(n).wait_recv()
        for m in range(4):
            pc[n, c, m] = pc[n, c, m] + cb[n, m]

    def fy(d, p):
        py = lax.rem(y + d, 4)
        return remote(pf.at[py, p], ryf.at[d - 1, p], fys, fyr, at(x, py, z, c))

    def fz(d):
        pz = lax.rem(z + d, 8)
        j, f = owned(pz, side)
        return remote(sf.at[2 * j + f], rzf.at[d - 1], fzs, fzr, at(x, y, pz, c))

    def ey(d):
        py = lax.rem(y + d, 4)
        return remote(pc.at[1, c, py], rye.at[d - 1], eys, eyr, at(x, py, z, c))

    def ez(d):
        pz = lax.rem(z + d, 8)
        j, f = owned(pz, side)
        return remote(se_.at[j, f], rze.at[d - 1], ezs, ezr, at(x, y, pz, c))

    def d_own(pz):
        j, f = owned(pz, 1 - side)
        return pc.at[0, c, :, j, f]

    def dz(d):
        pz = lax.rem(z + d, 8)
        return remote(d_own(pz), rzd.at[d - 1], dzs, dzr, at(x, y, pz, c))

    def dy(d):
        py = lax.rem(y + d, 4)
        return remote(sd.at[py], ryd.at[d - 1], dys, dyr, at(x, py, z, c))

    def deliver(n):
        dev, src, dst, sem = outgoing[n]
        return remote(src, dst, fs.at[n], sem, dev)

    def send_out(n):
        dev, src, dst, _ = outgoing[n]

        @pl.when(jnp.logical_not(is_me(dev)))
        def _():
            deliver(n).start()

        if n < 2:
            @pl.when(is_me(dev))
            def _():
                pltpu.make_async_copy(src, dst, outgoing[n][3]).start()

    def f_piece(p, k):
        rows = pl.ds(pl.multiple_of(p * 128, 128), 128)
        for n in range(2):
            whole(p, k, n).wait_recv()
            turn(xfull, 1, p, n)
            part = slice(n * 384, (n + 1) * 384)
            value = dot3(gg[0, 0, :, part], gg[0, 1, :, part], gg[1, 0, rows, part], gg[1, 1, rows, part], NT_DIMS)
            for m in range(4):
                block = value[m * 128:(m + 1) * 128].reshape(2, 64, 128)
                pf[m, p] = block if n == 0 else pf[m, p] + block
        for d in (2, 1, 3):
            fy(d, p).start()

    pair = hi * 2

    def f_row(m):
        rows = pl.ds(pl.multiple_of(m * 128, 128), 128)
        cols = pl.ds(pl.multiple_of(pair * 128, 256), 256)
        value = dot3(gg[0, 0, rows, :], gg[0, 1, rows, :], gg[1, 0, cols, :], gg[1, 1, cols, :], NT_DIMS)
        for n in range(2):
            pf[m, pair + n] = value[:, n * 128:(n + 1) * 128].reshape(2, 64, 128)
        d = lax.rem(m + 4 - y, 4)

        @pl.when(d > 0)
        def _():
            for n in range(2):
                fy(d, pair + n).start()

    def half_out(k, n):
        hb[k, 3 * n:3 * n + 3] = half_of(peers[k], n)
        swap(k, n).start()

    def half_own(n):
        blk[3 * n:3 * n + 3, i] = half_of(i, n)
        whole(i, 3, n).start()

        @pl.when(mine == n)
        def _():
            part_way(i).start()


    def arrived(k, n):
        swap_in(k, n).wait_recv()
        whole(peers[k], k, n).start()

    take_c(0)
    half_out(0, 0)
    half_own(0)
    half_out(2, 0)
    take_c(1)
    half_out(0, 1)
    half_own(1)
    arrived(2, 0)
    half_out(1, 0)
    half_out(2, 1)
    half_out(1, 1)
    turn(blk, 0, i)
    arrived(2, 1)
    turn(blk, 0, peers[2])
    arrived(0, 0)
    arrived(0, 1)
    turn(blk, 0, peers[0])
    get_whole(i, 3)
    get_whole(peers[2], 2)
    part_way(peers[2]).start()
    f_row(i)
    f_row(peers[2])
    f_row(peers[0])
    arrived(1, 0)
    part_way(peers[0]).start()
    arrived(1, 1)
    turn(blk, 0, peers[1])
    part_way(peers[1]).start()
    square(0, gg, 0, 0)
    core_swap(0).start()
    f_row(peers[1])
    core_sum(0)
    for d in (4, 3, 5, 2, 6, 1, 7):
        dz(d).start()
    f_piece(peers[0], 0)
    f_piece(peers[1], 1)
    turn_half(xfull, 3 * others, 1 - c)
    took(xr.at[8], xhalf)
    turn_half(xhalf, 0, c)
    square(1, eh, 0, 1)
    core_swap(1).start()
    core_sum(1)
    for d in (2, 1, 3):
        ey(d).start()
    took(fyr, ryf)
    for m in range(4):
        sf[2 * m:2 * m + 2] = pf[y, m] + ryf[0, m] + ryf[1, m] + ryf[2, m]
    for d in (4, 3, 5, 2, 6, 1, 7):
        fz(d).start()
    took(eyr, rye)
    se_[...] = pc[1, c, y] + rye[0] + rye[1] + rye[2]
    for d in (4, 3, 5, 2, 6, 1, 7):
        ez(d).start()
    took(dzr, rzd)
    total = d_own(z)[...]
    for d in range(7):
        total = total + rzd[d]
    sd[...] = total
    for d in (2, 1, 3):
        dy(d).start()
    took(fzr, rzf)
    total = sf[2 * bj + sub]
    for d in range(7):
        total = total + rzf[d]
    redf[...] = total
    send_out(1)
    send_out(2)
    took(dyr, ryd)
    redq[0] = sd[y] + ryd[0] + ryd[1] + ryd[2]
    send_out(0)
    took(ezr, rze)
    total = se_[bj, sub]
    for d in range(7):
        total = total + rze[d]
    redq[1] = total
    send_out(3)
    send_out(4)

    @pl.when(delta == 0)
    def _():
        took(frq.at[0], fin_q.at[0])
        out_ref[...] = fin_q[0].reshape(128, 128)

    @pl.when(turned)
    def _():
        took(frq.at[0], fin_q.at[0])
        took(frq.at[1], fin_q.at[1])
        out_ref[...] = fin_q[0].reshape(128, 128) + fin_q[1].reshape(128, 128).T

    @pl.when(odd)
    def _():
        took(frf.at[0], fin_f.at[0])
        took(frf.at[1], fin_f.at[1])
        out_ref[...] = fin_f[0].reshape(128, 128) + fin_f[1].reshape(128, 128).T

    for sem, ref in (
        (c1s, tslice.at[pl.ds(0, 15)]), (tis, tall.at[pl.ds(0, 15)]), (c2s, picks), (has, hb),
        (xs.at[0], blk), (xs.at[1], xhalf), (ccs, cb), (fys, ryf), (fzs, rzf), (eys, rye), (ezs, rze), (dzs, rzd), (dys, ryd),
    ):
        took(sem, ref)
    for n in range(5):
        @pl.when(jnp.logical_not(is_me(outgoing[n][0])))
        def _():
            deliver(n).wait_send()


def on_device(three_index, coefficients, tile_index):
    dma = pltpu.SemaphoreType.DMA
    vm = pltpu.VMEM
    return pl.pallas_call(
        kernel,
        out_shape=jax.ShapeDtypeStruct((128, 128), F32),
        in_specs=[
            pl.BlockSpec(memory_space=pl.ANY),
            pl.BlockSpec(memory_space=pl.ANY),
            pl.BlockSpec(memory_space=pl.ANY),
        ],
        out_specs=pl.BlockSpec(memory_space=pltpu.VMEM),
        scratch_shapes=[
            vm((1536, 512), F32), vm((1536, 512), BF16), vm((1536, 512), BF16),
            vm((16, 8, 256), F32), vm((8, 128), jnp.int32), vm((16, 8, 128), jnp.int32),
            pltpu.SMEM((16, 128), jnp.int32), pltpu.SMEM((1, 4), jnp.int32),
            vm((15, 2, 4, 8, 128), F32), vm((2, 4, 16, 8, 128), F32),
            vm((512, 256), BF16), vm((512, 256), BF16),
            vm((3, 6, 128, 128), F32), vm((6, 4, 128, 128), F32), vm((6, 4, 128, 128), F32), vm((3, 4, 128, 128), F32),
            vm((2, 2, 512, 768), BF16), vm((2, 2, 512, 384), BF16),
            vm((2, 2, 4, 4, 2, 32, 128), F32), vm((2, 4, 4, 2, 32, 128), F32),
            vm((4, 4, 2, 64, 128), F32), vm((3, 4, 2, 64, 128), F32), vm((8, 64, 128), F32), vm((7, 64, 128), F32),
            vm((64, 128), F32),
            vm((3, 4, 2, 32, 128), F32), vm((4, 2, 32, 128), F32), vm((7, 32, 128), F32),
            vm((7, 4, 32, 128), F32), vm((4, 32, 128), F32), vm((3, 32, 128), F32),
            vm((2, 32, 128), F32), vm((2, 2, 2, 32, 128), F32), vm((2, 2, 64, 128), F32),
            dma((3,)), dma, dma, dma, dma, dma, dma((2,)), dma,
            dma, dma((6,)), dma((2,)), dma((9,)), dma, dma((2,)),
            dma, dma, dma, dma, dma, dma, dma, dma, dma, dma, dma, dma,
            dma((5,)), dma((2,)), dma((2,)),
        ],
        compiler_params=pltpu.CompilerParams(
            collective_id=0, has_side_effects=True, vmem_limit_bytes=55091 * 2**10
        ),
    )(three_index.reshape(1536, 512), coefficients.reshape(16, 8, 256), tile_index)


def solution(mesh):
    return jax.shard_map(
        on_device,
        mesh=mesh,
        in_specs=(P("aux", "row", None), P("aux", None), P("aux", "row", None)),
        out_specs=P("row", "aux"),
        check_vma=False,
    )
```
